128 devices in a mesh: rows: 8 (over z, core), cols: 16 (over y, x).
Axes of the slice: x: 4, y: 4, z: 4, core: 2. Of those that a mesh axis runs over, the one named last changes fastest.
Arguments:
- row_bases: bfloat16 [32, 128, 2048], P('rows', None, 'cols'), may hold values from -6 to 6
- col_bases: bfloat16 [768, 128, 2048], P('cols', None, 'rows'), may hold values from -6 to 6
- test_matrix: bfloat16 [768, 64, 2048], P('cols', None, 'rows'), may hold values from -6 to 6
- couplings: bfloat16 [8192, 64, 128], P(('rows', 'cols')), may hold values from -6 to 6
- tile_rows: int32 [8192], P(('rows', 'cols')), may hold values from 0 to 4, as said below
- tile_cols: int32 [8192], P(('rows', 'cols')), may hold values from 0 to 767, as said below
Outputs:
- new_basis: float32 [32, 64, 2048], P('rows', None, 'cols')
- new_couplings: float32 [8192, 64, 128], P(('rows', 'cols'))
The draws below stay inside these ranges and needn't reach their ends.
Inputs may be any that keep to these rules, and one draw needn't show every extreme that they name: `tile_rows`: the 64 slots of one device hold the tiles of block rows of its own row group only; they are 4-slot buckets in order, bucket k holding only block columns kept on cols index k; live slots of a bucket come first. In every row group some bucket index is full on every device, and every block row of the slab has live tiles. `tile_cols`: in bucket k of any device the block column lies in k * 48 to (k + 1) * 48 - 1, empty slots too.
All inputs are finite; a program needn't handle non-finite values.
Results may differ from the reference program's by a relative error of at most 0.0003.
Values may be sent and summed in bfloat16 or wider, within the bound.
A program may use at most 128 MiB of HBM per device.

```python
import math
import jax
import jax.numpy as jnp
from jax import lax

RANK = 64
LEAF = 2048
BR_DEV = 4
CB_DEV = 48
BUCKET = 4
NBC = 768
BROWS = 32
TILES = 8192
N_ROWS = 8
N_COLS = 16


def tile_layout(key):
    shape = (N_ROWS, N_COLS, N_COLS, BUCKET)
    keys = jax.random.split(key, 5)
    counts = jax.random.randint(keys[0], (N_ROWS, N_COLS, N_COLS, 1), 1, BUCKET + 1)
    busiest = jax.random.randint(keys[1], (N_ROWS, 1, 1, 1), 0, N_COLS)
    target = jnp.arange(N_COLS, dtype=jnp.int32).reshape(1, 1, N_COLS, 1)
    counts = jnp.where(target == busiest, BUCKET, counts)
    slot = jnp.arange(BUCKET, dtype=jnp.int32).reshape(1, 1, 1, BUCKET)
    offset = jax.random.randint(keys[2], (N_ROWS, N_COLS, N_COLS, 1), 0, BR_DEV)
    spread = jax.random.randint(keys[3], shape, 0, BR_DEV)
    rows = jnp.where(slot < BR_DEV, (slot + offset) % BR_DEV, spread)
    rows = jnp.where(slot < counts, rows, BR_DEV)
    cols = target * CB_DEV + jax.random.randint(keys[4], shape, 0, CB_DEV)
    return (rows.reshape(-1).astype(jnp.int32), cols.reshape(-1).astype(jnp.int32))


def draw_tile_rows(key, part):
    rows, cols = tile_layout(key)
    return rows


def draw_tile_cols(key, part):
    rows, cols = tile_layout(key)
    return cols


def level_of(rng, dims, shards, least, top_value):
    loudness, own = 1.0, jax.random.fold_in(rng, 6)
    for position, shards_of in shards:
        draws = jnp.exp(jax.random.uniform(jax.random.fold_in(own, position), (shards_of,), jnp.float32, least / len(shards), top_value / len(shards)))
        loudness = loudness * jnp.repeat(draws, dims[position] // shards_of).reshape([-1 if axis == position else 1 for axis in range(len(dims))])
    return loudness


def normal_values(rng, dims, deviation, most, shards=(), kind=jnp.bfloat16):
    gain = level_of(rng, dims, shards, -0.22, 0.18) if shards else 1.0
    entries = jax.random.normal(rng, dims, jnp.float32) * deviation * gain
    return jnp.minimum(jnp.maximum(entries, -most), most).astype(kind)


def setup_inputs(seed: int = 0) -> dict:
    streams_of = jax.random.split(jax.random.key(seed), 7)
    return {
        "row_bases": normal_values(streams_of[0], (BROWS, 2 * RANK, LEAF), 1.0, 6.0, ((0, 8), (2, 16))),
        "col_bases": normal_values(streams_of[1], (NBC, 2 * RANK, LEAF), 1.0, 6.0, ((0, 16), (2, 8))),
        "test_matrix": normal_values(streams_of[2], (NBC, RANK, LEAF), 1.0, 6.0, ((0, 16), (2, 8))),
        "couplings": normal_values(streams_of[3], (TILES, RANK, 2 * RANK), 1.0, 6.0, ((0, 128),)),
        "tile_rows": draw_tile_rows(jax.random.fold_in(streams_of[6], 71), 0),
        "tile_cols": draw_tile_cols(jax.random.fold_in(streams_of[6], 71), 0),
    }


def tile_terms(picked, couplings, weights, sketch_width):
    upper_limit = lax.Precision.HIGHEST
    first_operator = jnp.einsum('tak,tbk->tab', picked[:, :, :sketch_width], couplings[:, :, :sketch_width], precision=upper_limit)
    second_operator = jnp.einsum('tak,tbk->tab', picked[:, :, sketch_width:], couplings[:, :, sketch_width:], precision=upper_limit)
    terms = jnp.concatenate([first_operator, second_operator], axis=2)
    return jnp.einsum('ti,tab->iab', weights, terms, precision=upper_limit)

def reference(row_bases, col_bases, test_matrix, couplings, tile_rows, tile_cols):
    upper_limit = lax.Precision.HIGHEST
    sketch_width = test_matrix.shape[1]

    def sketch_one(pair):
        return jnp.dot(pair[0].astype(jnp.float32), pair[1].astype(jnp.float32).T, precision=upper_limit)
    sketch = lax.map(sketch_one, (test_matrix, col_bases)) / math.sqrt(LEAF)
    per_group = BUCKET * N_COLS * N_COLS
    group = jnp.arange(TILES, dtype=jnp.int32) // per_group
    rows_all = jnp.where(tile_rows < BR_DEV, group * BR_DEV + tile_rows, BROWS).astype(jnp.int32)
    weights = (rows_all[:, None] == jnp.arange(BROWS, dtype=jnp.int32)[None, :]).astype(jnp.float32)
    picked = jnp.take(sketch, tile_cols, axis=0).astype(jnp.float32)
    coupled_matrix = couplings.astype(jnp.float32)
    row_side_sketch = tile_terms(picked, coupled_matrix, weights, sketch_width)
    bases32 = row_bases.astype(jnp.float32)
    gram = jnp.einsum('ikl,iml->ikm', bases32, bases32, precision=upper_limit) / LEAF
    middle_factor = jnp.einsum('iab,ibc->iac', row_side_sketch, gram, precision=upper_limit)
    curvature_factor = jnp.einsum('jgy,jsy->jgs', middle_factor, row_side_sketch, precision=upper_limit)
    lower = jnp.linalg.cholesky(curvature_factor)
    coeff = jax.vmap(lambda a, b: jax.scipy.linalg.solve_triangular(a, b, lower=True))(lower, row_side_sketch)
    new_basis = jnp.einsum('iak,ikl->ial', coeff, bases32, precision=upper_limit)
    projected = jnp.einsum('iab,ibc->iac', coeff, gram, precision=upper_limit)
    selected_columns = jnp.einsum('ti,iab->tab', weights, projected, precision=upper_limit)
    first_operator = jnp.einsum('zdp,zpv->zdv', selected_columns[:, :, :sketch_width], coupled_matrix[:, :, :sketch_width], precision=upper_limit)
    second_operator = jnp.einsum('zdp,zpv->zdv', selected_columns[:, :, sketch_width:], coupled_matrix[:, :, sketch_width:], precision=upper_limit)
    new_couplings = jnp.concatenate([first_operator, second_operator], axis=2)
    return (new_basis, new_couplings)
```

```python
import functools
import math

import jax
import jax.numpy as jnp
from jax import lax
from jax.experimental import pallas as pl
from jax.experimental.pallas import tpu as pltpu
from jax.sharding import PartitionSpec as P

MESH = pl.DeviceIdType.MESH
F32 = jnp.float32
BF16 = jnp.bfloat16
LEAF = 2048
SCALE = 1.0 / math.sqrt(LEAF)
CB = 48
HALF = 24
CH = 6
HC = 3
NCOL = 16
NT = (((1,), (1,)), ((), ()))
NN = (((1,), (0,)), ((), ()))
OFFSETS = [(dy, dx) for dy in range(4) for dx in range(4) if (dy, dx) != (0, 0)]


def split_hi_lo(value):
    hi = value.astype(BF16)
    return hi, (value - hi.astype(F32)).astype(BF16)


def front_kernel(
    cb, tm, cp, rb, idx, out_r, out_g,
    cbv, tmv, rbv, part, own, prx, zr1, zr2, full, cpl, idxv, idxs,
    gpart, grx, gall, rpart, rrx, rall,
    ld_sem, misc_sem, pc_send, pc_recv, zs_send, zs_recv, ag_send, ag_recv, fw_send, fw_recv,
    cp_send, cp_recv, ix_send, ix_recv, g1_send, g1_recv, g2_send, g2_recv,
    r1_send, r1_recv, r2_send, r2_recv,
):
    r = lax.axis_index("rows")
    k = lax.axis_index("cols")
    z, h = lax.div(r, 2), lax.rem(r, 2)
    y, x = lax.div(k, 4), lax.rem(k, 4)
    partner = (r + 1 - 2 * h, k)
    up = (lax.rem(z + 1, 4) * 2 + h, k)
    down = (lax.rem(z + 3, 4) * 2 + h, k)
    peers = [lax.rem(y + dy, 4) * 4 + lax.rem(x + dx, 4) for dy, dx in OFFSETS]

    def zc(q):
        return lax.rem(z + q, 4) * CH

    order = (2, 1, 3, 0)
    loads = {}
    for n, half in enumerate((1 - h, h)):
        for m, q in enumerate(order):
            at = pl.ds(half * HALF + zc(q), CH)
            a = pltpu.make_async_copy(cb.at[at], cbv.at[at], ld_sem.at[0, n * 4 + m])
            b = pltpu.make_async_copy(tm.at[at], tmv.at[at], ld_sem.at[1, n * 4 + m])
            a.start()
            b.start()
            loads[n, q] = (a, b)
    load_rb = pltpu.make_async_copy(rb, rbv, misc_sem.at[0])
    load_rb.start()
    own_cp = pltpu.make_async_copy(cp.at[pl.ds(4 * k, 4)], cpl.at[k], misc_sem.at[1])
    own_cp.start()
    own_ix = pltpu.make_async_copy(idx, idxv.at[k], misc_sem.at[2])
    own_ix.start()

    barrier = pltpu.get_barrier_semaphore()
    for device in [partner, up, down] + [(r, c) for c in peers]:
        pl.semaphore_signal(barrier, inc=1, device_id=device, device_id_type=MESH)

    def sketch(n, q, dst):
        for load in loads[n, q]:
            load.wait()
        half = (1 - h) if n == 0 else h
        base = half * HALF + zc(q)

        @pl.loop(0, CH, unroll=True)
        def _(u):
            dst[zc(q) + u] = (
                lax.dot_general(tmv[base + u], cbv[base + u], NT, preferred_element_type=F32) * SCALE
            )

    def remote(src, dst, send, recv, device):
        return pltpu.make_async_remote_copy(
            src_ref=src, dst_ref=dst, send_sem=send, recv_sem=recv, device_id=device, device_id_type=MESH
        )

    started = []

    def go(copy):
        copy.start()
        started.append(copy)
        return copy

    sketch(0, 2, part)
    pl.semaphore_wait(barrier, 3 + len(OFFSETS))
    to_partner = {}

    def send_partner(m, q):
        at = pl.ds(zc(q), CH)
        to_partner[q] = go(remote(part.at[at], prx.at[at], pc_send.at[m], pc_recv.at[m], partner))

    send_partner(0, 2)
    moves = []
    for n, c in enumerate(peers):
        moves.append((
            go(remote(cp.at[pl.ds(4 * c, 4)], cpl.at[k], cp_send.at[n], cp_recv.at[n], (r, c))),
            go(remote(idx, idxv.at[k], ix_send.at[n], ix_recv.at[n], (r, c))),
        ))
    for m, q in enumerate(order):
        if m:
            sketch(0, q, part)
            send_partner(m, q)

    def add_partner(q):
        sketch(1, q, own)
        to_partner[q].wait_recv()
        at = pl.ds(zc(q), CH)
        own[at] = own[at] + prx[at]

    add_partner(2)
    a2 = go(remote(own.at[pl.ds(zc(2), HC)], zr1.at[0], zs_send.at[0], zs_recv.at[0], up))
    b2 = go(remote(own.at[pl.ds(zc(2) + HC, HC)], zr1.at[1], zs_send.at[1], zs_recv.at[1], down))
    add_partner(1)
    b1 = go(remote(own.at[pl.ds(zc(1) + HC, HC)], zr2.at[1], zs_send.at[2], zs_recv.at[2], up))
    add_partner(3)
    a3 = go(remote(own.at[pl.ds(zc(3), HC)], zr2.at[2], zs_send.at[3], zs_recv.at[3], down))
    add_partner(0)

    load_rb.wait()
    for i in range(4):
        gpart[:, pl.ds(i * 128, 128)] = lax.dot_general(rbv[i], rbv[i], NT, preferred_element_type=F32) * (1.0 / LEAF)
    gram1 = [
        go(remote(gpart.at[pl.ds(8 * c, 8)], grx.at[n], g1_send.at[n], g1_recv.at[n], (r, c)))
        for n, c in enumerate(peers)
    ]

    a2.wait_recv()
    at = pl.ds(zc(1), HC)
    own[at] = own[at] + zr1[0]
    a1 = go(remote(own.at[at], zr2.at[0], zs_send.at[4], zs_recv.at[4], up))
    b2.wait_recv()
    at = pl.ds(zc(3) + HC, HC)
    own[at] = own[at] + zr1[1]
    b3 = go(remote(own.at[at], zr2.at[3], zs_send.at[5], zs_recv.at[5], down))

    for copy in gram1:
        copy.wait_recv()
    total = gpart[pl.ds(pl.multiple_of(8 * k, 8), 8)]
    for n in range(len(OFFSETS)):
        total = total + grx[n]
    gall[k] = total
    gram2 = [
        go(remote(gall.at[k], gall.at[k], g2_send.at[n], g2_recv.at[n], (r, c)))
        for n, c in enumerate(peers)
    ]

    for copy in (b1, a3, a1, b3):
        copy.wait_recv()
    mine = h * HALF + zc(0)
    at = pl.ds(zc(0), HC)
    full[pl.ds(mine, HC)] = own[at] + zr2[0] + zr2[2]
    at = pl.ds(zc(0) + HC, HC)
    full[pl.ds(mine + HC, HC)] = own[at] + zr2[1] + zr2[3]

    def spread(start, count, send, recv, device):
        at = pl.ds(start, count)
        return go(remote(full.at[at], full.at[at], send, recv, device))

    g_up = spread(mine, CH, ag_send.at[0], ag_recv.at[0], up)
    g_down = spread(mine, CH, ag_send.at[1], ag_recv.at[1], down)
    forwarded = [spread(mine, CH, fw_send.at[0], fw_recv.at[0], partner)]
    g_up.wait_recv()
    below = h * HALF + zc(3)
    f_up = spread(below, HC, ag_send.at[2], ag_recv.at[2], up)
    forwarded.append(spread(below, CH, fw_send.at[1], fw_recv.at[1], partner))
    g_down.wait_recv()
    above = h * HALF + zc(1)
    f_down = spread(above + HC, HC, ag_send.at[3], ag_recv.at[3], down)
    forwarded.append(spread(above, CH, fw_send.at[2], fw_recv.at[2], partner))
    far = h * HALF + zc(2)
    f_up.wait_recv()
    forwarded.append(spread(far, HC, fw_send.at[3], fw_recv.at[3], partner))
    f_down.wait_recv()
    forwarded.append(spread(far + HC, HC, fw_send.at[4], fw_recv.at[4], partner))

    own_cp.wait()
    own_ix.wait()
    for a, b in moves:
        a.wait_recv()
        b.wait_recv()
    to_scalars = pltpu.make_async_copy(idxv, idxs, misc_sem.at[3])
    to_scalars.start()
    to_scalars.wait()
    for copy in forwarded:
        copy.wait_recv()

    first = lax.broadcasted_iota(jnp.int32, (64, 128), 1) < 64

    def tiles(c, carry):
        sums = list(carry)
        for s in range(4):
            j = jnp.clip(idxs[c, 0, 4 * k + s] - CB * k, 0, CB - 1)
            row = idxs[c, 0, 64 + 4 * k + s]
            hi, lo = split_hi_lo(full[j])
            coupling = cpl[c, s].astype(F32)
            zero = jnp.zeros_like(coupling)
            pair = jnp.concatenate(
                [jnp.where(first, coupling, zero), jnp.where(first, zero, coupling)], axis=0
            ).astype(BF16)
            both = lax.dot_general(jnp.concatenate([hi, lo], axis=0), pair, NT, preferred_element_type=F32)
            term = both[:64] + both[64:]
            for i in range(4):
                sums[i] = sums[i] + jnp.where(row == i, 1.0, 0.0) * term
        return tuple(sums)

    sums = lax.fori_loop(0, NCOL, tiles, (jnp.zeros((64, 128), F32),) * 4)
    for i in range(4):
        rpart[pl.ds(4 * i, 4)] = sums[i].reshape(4, 16, 128)

    row1 = [
        go(remote(rpart.at[c], rrx.at[n], r1_send.at[n], r1_recv.at[n], (r, c)))
        for n, c in enumerate(peers)
    ]
    for copy in row1:
        copy.wait_recv()
    total = rpart[k]
    for n in range(len(OFFSETS)):
        total = total + rrx[n]
    rall[k] = total
    row2 = [
        go(remote(rall.at[k], rall.at[k], r2_send.at[n], r2_recv.at[n], (r, c)))
        for n, c in enumerate(peers)
    ]
    for copy in gram2:
        copy.wait_recv()
    for c in range(NCOL):
        for i in range(4):
            out_g[i, pl.ds(8 * c, 8)] = gall[c, :, pl.ds(128 * i, 128)]
    for copy in row2:
        copy.wait_recv()
    out_r[...] = rall[...]
    for copy in started:
        copy.wait_send()


def front(cb, tm, cp, rb, idx):
    any_space = pl.BlockSpec(memory_space=pl.ANY)
    vmem = pl.BlockSpec(memory_space=pltpu.VMEM)
    dma = pltpu.SemaphoreType.DMA
    peers = len(OFFSETS)
    return pl.pallas_call(
        front_kernel,
        out_shape=(
            jax.ShapeDtypeStruct((NCOL, 16, 128), F32),
            jax.ShapeDtypeStruct((4, 128, 128), F32),
        ),
        in_specs=[any_space] * 5,
        out_specs=(vmem, vmem),
        scratch_shapes=[
            pltpu.VMEM((CB, 128, 256), BF16),
            pltpu.VMEM((CB, 64, 256), BF16),
            pltpu.VMEM((4, 128, 128), BF16),
            pltpu.VMEM((HALF, 64, 128), F32),
            pltpu.VMEM((HALF, 64, 128), F32),
            pltpu.VMEM((HALF, 64, 128), F32),
            pltpu.VMEM((2, HC, 64, 128), F32),
            pltpu.VMEM((4, HC, 64, 128), F32),
            pltpu.VMEM((CB, 64, 128), F32),
            pltpu.VMEM((NCOL, 4, 64, 128), BF16),
            pltpu.VMEM((NCOL, 8, 128), jnp.int32),
            pltpu.SMEM((NCOL, 8, 128), jnp.int32),
            pltpu.VMEM((128, 512), F32),
            pltpu.VMEM((peers, 8, 512), F32),
            pltpu.VMEM((NCOL, 8, 512), F32),
            pltpu.VMEM((NCOL, 16, 128), F32),
            pltpu.VMEM((peers, 16, 128), F32),
            pltpu.VMEM((NCOL, 16, 128), F32),
            dma((2, 8)), dma((4,)),
            dma((4,)), dma((4,)), dma((6,)), dma((6,)), dma((4,)), dma((4,)), dma((5,)), dma((5,)),
        ] + [dma((peers,))] * 12,
        compiler_params=pltpu.CompilerParams(
            collective_id=0, has_side_effects=True, vmem_limit_bytes=40 * 1024 * 1024
        ),
    )(cb, tm, cp, rb, idx)


def back_kernel(rows_s, r_ref, g_ref, rb, cp, nb, nc, cpv, rbv, ncv, proj, sem, out_sem):
    load_cp = pltpu.make_async_copy(cp, cpv, sem.at[0])
    load_cp.start()
    load_rb = pltpu.make_async_copy(rb, rbv, sem.at[1])
    load_rb.start()
    highest = lax.Precision.HIGHEST

    work_a, work_r = [], []
    for i in range(4):
        rs = r_ref[pl.ds(4 * i, 4)].reshape(64, 128)
        middle = lax.dot_general(rs, g_ref[i], NN, precision=highest, preferred_element_type=F32)
        a = lax.dot_general(middle, rs, NT, precision=highest, preferred_element_type=F32)
        work_a.append([a[8 * b:8 * b + 8] for b in range(8)])
        work_r.append([rs[8 * b:8 * b + 8] for b in range(8)])

    sub = lax.broadcasted_iota(jnp.int32, (8, 128), 0)
    for step in range(16):
        b, o = divmod(4 * step, 8)
        for i in range(4):
            a, rr = work_a[i], work_r[i]
            cols = [
                [jnp.broadcast_to(a[n][:, 4 * step + p:4 * step + p + 1], (8, 128)) for n in range(b, 8)]
                for p in range(4)
            ]
            ra = [a[b][o + p:o + p + 1] for p in range(4)]
            rw = [rr[b][o + p:o + p + 1] for p in range(4)]
            mult, ua, ur = [], [], []
            for p in range(4):
                col, va, vr = cols[p], ra[p], rw[p]
                for q in range(p):
                    l = mult[q][0][o + p:o + p + 1]
                    col = [cc - mm * l for cc, mm in zip(col, mult[q])]
                    va = va - l[:, :64] * ua[q]
                    vr = vr - l * ur[q]
                inv = lax.rsqrt(col[0][o + p:o + p + 1])
                mult.append([cc * inv for cc in col])
                ua.append(va * inv[:, :64])
                ur.append(vr * inv)
            below = sub >= o + 4
            for n in range(b, 8):
                if n == b and o == 4:
                    continue
                da = sum(mult[p][n - b][:, :64] * ua[p] for p in range(4))
                dr = sum(mult[p][n - b] * ur[p] for p in range(4))
                if n == b:
                    da = jnp.where(below[:, :64], da, 0.0)
                    dr = jnp.where(below, dr, 0.0)
                a[n] = a[n] - da
                rr[n] = rr[n] - dr
            fin = rr[b]
            for p in range(4):
                fin = jnp.where(sub == o + p, ur[p], fin)
            rr[b] = fin

    load_rb.wait()
    for i in range(4):
        coeff = jnp.concatenate(work_r[i], axis=0)
        hi, lo = split_hi_lo(coeff)
        basis = rbv[i]
        nb[i] = (
            lax.dot_general(hi, basis, NN, preferred_element_type=F32)
            + lax.dot_general(lo, basis, NN, preferred_element_type=F32)
        )
        p = lax.dot_general(coeff, g_ref[i], NN, precision=highest, preferred_element_type=F32)
        hi, lo = split_hi_lo(p)
        proj[i] = jnp.concatenate([hi, lo], axis=0)

    load_cp.wait()
    first = lax.broadcasted_iota(jnp.int32, (64, 128), 1) < 64
    outs = [pltpu.make_async_copy(ncv.at[pl.ds(8 * n, 8)], nc.at[pl.ds(8 * n, 8)], out_sem.at[n]) for n in range(8)]
    for n in range(8):
        for t in range(8 * n, 8 * n + 8):
            row = rows_s[t]
            coupling = cpv[t].astype(F32)
            zero = jnp.zeros_like(coupling)
            pair = jnp.concatenate(
                [jnp.where(first, coupling, zero), jnp.where(first, zero, coupling)], axis=0
            ).astype(BF16)
            both = lax.dot_general(proj[jnp.minimum(row, 3)], pair, NN, preferred_element_type=F32)
            live = jnp.where(row < 4, 1.0, 0.0)
            ncv[t] = (both[:64] + both[64:]) * live
        outs[n].start()
    for copy in outs:
        copy.wait()


def back(tile_rows, r_side, gram, rb, cp):
    any_space = pl.BlockSpec(memory_space=pl.ANY)
    vmem = pl.BlockSpec(memory_space=pltpu.VMEM)
    return pl.pallas_call(
        back_kernel,
        out_shape=(
            jax.ShapeDtypeStruct((4, 64, 128), F32),
            jax.ShapeDtypeStruct((64, 64, 128), F32),
        ),
        in_specs=[pl.BlockSpec(memory_space=pltpu.SMEM), vmem, vmem, any_space, any_space],
        out_specs=(vmem, any_space),
        scratch_shapes=[
            pltpu.VMEM((64, 64, 128), BF16),
            pltpu.VMEM((4, 128, 128), BF16),
            pltpu.VMEM((64, 64, 128), F32),
            pltpu.VMEM((4, 128, 128), BF16),
            pltpu.SemaphoreType.DMA((2,)),
            pltpu.SemaphoreType.DMA((8,)),
        ],
        compiler_params=pltpu.CompilerParams(vmem_limit_bytes=40 * 1024 * 1024),
    )(tile_rows, r_side, gram, rb, cp)


def local(row_bases, col_bases, test_matrix, couplings, tile_rows, tile_cols):
    idx = jnp.broadcast_to(jnp.concatenate([tile_cols, tile_rows])[None, :], (8, 128))
    r_side, gram = front(col_bases, test_matrix, couplings, row_bases, idx)
    return back(tile_rows, r_side, gram, row_bases, couplings)


def solution(mesh):
    in_specs = (
        P("rows", None, "cols"),
        P("cols", None, "rows"),
        P("cols", None, "rows"),
        P(("rows", "cols"), None, None),
        P(("rows", "cols")),
        P(("rows", "cols")),
    )
    out_specs = (P("rows", None, "cols"), P(("rows", "cols"), None, None))
    return jax.shard_map(local, mesh=mesh, in_specs=in_specs, out_specs=out_specs, check_vma=False)
```

```python
import functools
import math

import jax
import jax.numpy as jnp
from jax import lax
from jax.experimental import pallas as pl
from jax.experimental.pallas import tpu as pltpu
from jax.sharding import PartitionSpec as P

MESH = pl.DeviceIdType.MESH
F32 = jnp.float32
BF16 = jnp.bfloat16
LEAF = 2048
SCALE = 1.0 / math.sqrt(LEAF)
CB = 48
HALF = 24
CH = 6
HC = 3
NCOL = 16
NT = (((1,), (1,)), ((), ()))
NN = (((1,), (0,)), ((), ()))
OFFSETS = [(dy, dx) for dy in range(4) for dx in range(4) if (dy, dx) != (0, 0)]


def split_hi_lo(value):
    hi = value.astype(BF16)
    return hi, (value - hi.astype(F32)).astype(BF16)


def front_kernel(
    cb, tm, cp, rb, tcols, trows, out_r, out_g,
    cbv, tmv, rbv, part, own, prx, zrx, full, skb, cpl, pairs, idxv, idxs,
    gpart, grx, gall, rpart, rrx, rall,
    ld_sem, misc_sem, pc_send, pc_recv, zs_send, zs_recv, ag_send, ag_recv, fw_send, fw_recv,
    cp_send, cp_recv, ix_send, ix_recv, g1_send, g1_recv, g2_send, g2_recv,
    r1_send, r1_recv, r2_send, r2_recv,
):
    r = lax.axis_index("rows")
    k = lax.axis_index("cols")
    z, h = lax.div(r, 2), lax.rem(r, 2)
    y, x = lax.div(k, 4), lax.rem(k, 4)
    partner = (r + 1 - 2 * h, k)
    along = {q: (lax.rem(z + q, 4) * 2 + h, k) for q in (1, 2, 3)}
    peers = [lax.rem(y + dy, 4) * 4 + lax.rem(x + dx, 4) for dy, dx in OFFSETS]

    def piece(s, q):
        return lax.rem(z + q, 4) * CH + s * HC

    order = [(s, q) for s in (0, 1) for q in (2, 1, 3, 0)]
    loads = {}
    for n, half in enumerate((1 - h, h)):
        for m, (s, q) in enumerate(order):
            at = pl.ds(half * HALF + piece(s, q), HC)
            a = pltpu.make_async_copy(cb.at[at], cbv.at[at], ld_sem.at[0, n * 8 + m])
            b = pltpu.make_async_copy(tm.at[at], tmv.at[at], ld_sem.at[1, n * 8 + m])
            a.start()
            b.start()
            loads[n, s, q] = (a, b)
    load_rb = pltpu.make_async_copy(rb, rbv, misc_sem.at[0])
    load_rb.start()
    own_cp = pltpu.make_async_copy(cp.at[pl.ds(4 * k, 4)], cpl.at[k], misc_sem.at[1])
    own_cp.start()

    barrier = pltpu.get_barrier_semaphore()
    for device in [partner, along[1], along[2], along[3]] + [(r, c) for c in peers]:
        pl.semaphore_signal(barrier, inc=1, device_id=device, device_id_type=MESH)

    def sketch(n, s, q, dst):
        for load in loads[n, s, q]:
            load.wait()
        half = (1 - h) if n == 0 else h
        base = half * HALF + piece(s, q)
        for u in range(HC):
            dst[piece(s, q) + u] = (
                lax.dot_general(tmv[base + u], cbv[base + u], NT, preferred_element_type=F32) * SCALE
            )

    def remote(src, dst, send, recv, device):
        return pltpu.make_async_remote_copy(
            src_ref=src, dst_ref=dst, send_sem=send, recv_sem=recv, device_id=device, device_id_type=MESH
        )

    started = []

    def go(copy):
        copy.start()
        started.append(copy)
        return copy

    for s, q in order:
        sketch(0, s, q, part)
    idxv[k] = jnp.broadcast_to(jnp.concatenate([tcols[...], trows[...]], axis=1), (8, 128))
    pl.semaphore_wait(barrier, 4 + len(OFFSETS))
    to_partner = {}
    for m, (s, q) in enumerate(order):
        at = pl.ds(piece(s, q), HC)
        to_partner[s, q] = go(remote(part.at[at], prx.at[at], pc_send.at[m], pc_recv.at[m], partner))

    scatter = {}
    for s, q in order:
        sketch(1, s, q, own)
        to_partner[s, q].wait_recv()
        at = pl.ds(piece(s, q), HC)
        own[at] = own[at] + prx[at]
        if q:
            n = 3 * s + q - 1
            scatter[s, q] = go(remote(own.at[at], zrx.at[n], zs_send.at[n], zs_recv.at[n], along[q]))

    moves = []
    for n, c in enumerate(peers):
        moves.append((
            go(remote(cp.at[pl.ds(4 * c, 4)], cpl.at[k], cp_send.at[n], cp_recv.at[n], (r, c))),
            go(remote(idxv.at[k], idxv.at[k], ix_send.at[n], ix_recv.at[n], (r, c))),
        ))

    load_rb.wait()
    for i in range(4):
        gpart[:, pl.ds(i * 128, 128)] = lax.dot_general(rbv[i], rbv[i], NT, preferred_element_type=F32) * (1.0 / LEAF)
    gram1 = [
        go(remote(gpart.at[pl.ds(8 * c, 8)], grx.at[n], g1_send.at[n], g1_recv.at[n], (r, c)))
        for n, c in enumerate(peers)
    ]

    def spread(start, send, recv, device):
        at = pl.ds(start, HC)
        return go(remote(full.at[at], full.at[at], send, recv, device))

    def halves(start):
        for u in range(HC):
            hi, lo = split_hi_lo(full[start + u])
            skb[start + u] = jnp.concatenate([hi, lo], axis=0)

    gather, forwarded = {}, []
    for s in (0, 1):
        for q in (1, 2, 3):
            scatter[s, q].wait_recv()
        mine = h * HALF + piece(s, 0)
        full[pl.ds(mine, HC)] = own[pl.ds(piece(s, 0), HC)] + zrx[3 * s] + zrx[3 * s + 1] + zrx[3 * s + 2]
        for q in (2, 1, 3):
            n = 3 * s + q - 1
            gather[s, q] = spread(mine, ag_send.at[n], ag_recv.at[n], along[q])
        forwarded.append((s, 0, spread(mine, fw_send.at[4 * s], fw_recv.at[4 * s], partner)))
        halves(mine)

    for copy in gram1:
        copy.wait_recv()
    total = gpart[pl.ds(pl.multiple_of(8 * k, 8), 8)]
    for n in range(len(OFFSETS)):
        total = total + grx[n]
    gall[k] = total
    gram2 = [
        go(remote(gall.at[k], gall.at[k], g2_send.at[n], g2_recv.at[n], (r, c)))
        for n, c in enumerate(peers)
    ]

    for s in (0, 1):
        for q in (1, 3, 2):
            gather[s, q].wait_recv()
            n = 4 * s + q
            start = h * HALF + piece(s, 4 - q)
            forwarded.append((s, 4 - q, spread(start, fw_send.at[n], fw_recv.at[n], partner)))
            halves(start)

    own_cp.wait()
    for a, b in moves:
        a.wait_recv()
        b.wait_recv()
    to_scalars = pltpu.make_async_copy(idxv, idxs, misc_sem.at[2])
    to_scalars.start()
    first = lax.broadcasted_iota(jnp.int32, (64, 128), 1) < 64

    @pl.loop(0, NCOL)
    def _(c):
        for s in range(4):
            coupling = cpl[c, s].astype(F32)
            zero = jnp.zeros_like(coupling)
            pairs[4 * c + s] = jnp.concatenate(
                [jnp.where(first, coupling, zero), jnp.where(first, zero, coupling)], axis=0
            ).astype(BF16)

    to_scalars.wait()
    for s, q, copy in forwarded:
        copy.wait_recv()
        halves((1 - h) * HALF + piece(s, q))

    def tiles(n, carry):
        sums = list(carry)
        for m in range(8):
            c, s = 2 * n + m // 4, m % 4
            j = jnp.clip(idxs[c, 0, 4 * k + s] - CB * k, 0, CB - 1)
            row = idxs[c, 0, 64 + 4 * k + s]
            both = lax.dot_general(skb[j], pairs[4 * c + s], NT, preferred_element_type=F32)
            term = both[:64] + both[64:]
            for i in range(4):
                sums[i] = sums[i] + jnp.where(row == i, 1.0, 0.0) * term
        return tuple(sums)

    sums = lax.fori_loop(0, NCOL // 2, tiles, (jnp.zeros((64, 128), F32),) * 4)
    for i in range(4):
        rpart[pl.ds(4 * i, 4)] = sums[i].reshape(4, 16, 128)

    row1 = [
        go(remote(rpart.at[c], rrx.at[n], r1_send.at[n], r1_recv.at[n], (r, c)))
        for n, c in enumerate(peers)
    ]
    for copy in gram2:
        copy.wait_recv()
    for c in range(NCOL):
        for i in range(4):
            out_g[i, pl.ds(8 * c, 8)] = gall[c, :, pl.ds(128 * i, 128)]
    for copy in row1:
        copy.wait_recv()
    total = rpart[k]
    for n in range(len(OFFSETS)):
        total = total + rrx[n]
    rall[k] = total
    row2 = [
        go(remote(rall.at[k], rall.at[k], r2_send.at[n], r2_recv.at[n], (r, c)))
        for n, c in enumerate(peers)
    ]
    for copy in row2:
        copy.wait_recv()
    out_r[...] = rall[...]
    for copy in started:
        copy.wait_send()


def front(cb, tm, cp, rb, tcols, trows):
    any_space = pl.BlockSpec(memory_space=pl.ANY)
    vmem = pl.BlockSpec(memory_space=pltpu.VMEM)
    dma = pltpu.SemaphoreType.DMA
    peers = len(OFFSETS)
    return pl.pallas_call(
        front_kernel,
        out_shape=(
            jax.ShapeDtypeStruct((NCOL, 16, 128), F32),
            jax.ShapeDtypeStruct((4, 128, 128), F32),
        ),
        in_specs=[any_space] * 4 + [vmem] * 2,
        out_specs=(vmem, vmem),
        scratch_shapes=[
            pltpu.VMEM((CB, 128, 256), BF16),
            pltpu.VMEM((CB, 64, 256), BF16),
            pltpu.VMEM((4, 128, 128), BF16),
            pltpu.VMEM((HALF, 64, 128), F32),
            pltpu.VMEM((HALF, 64, 128), F32),
            pltpu.VMEM((HALF, 64, 128), F32),
            pltpu.VMEM((6, HC, 64, 128), F32),
            pltpu.VMEM((CB, 64, 128), F32),
            pltpu.VMEM((CB, 128, 128), BF16),
            pltpu.VMEM((NCOL, 4, 64, 128), BF16),
            pltpu.VMEM((64, 128, 128), BF16),
            pltpu.VMEM((NCOL, 8, 128), jnp.int32),
            pltpu.SMEM((NCOL, 8, 128), jnp.int32),
            pltpu.VMEM((128, 512), F32),
            pltpu.VMEM((peers, 8, 512), F32),
            pltpu.VMEM((NCOL, 8, 512), F32),
            pltpu.VMEM((NCOL, 16, 128), F32),
            pltpu.VMEM((peers, 16, 128), F32),
            pltpu.VMEM((NCOL, 16, 128), F32),
            dma((2, 16)), dma((3,)),
            dma((8,)), dma((8,)), dma((6,)), dma((6,)), dma((6,)), dma((6,)), dma((8,)), dma((8,)),
        ] + [dma((peers,))] * 12,
        compiler_params=pltpu.CompilerParams(
            collective_id=0, has_side_effects=True, vmem_limit_bytes=60 * 1024 * 1024
        ),
    )(cb, tm, cp, rb, tcols, trows)


def back_kernel(rows_s, r_ref, g_ref, rb, cp, nb, nc, cpv, rbv, ncv, proj, sem, out_sem):
    load_cp = pltpu.make_async_copy(cp, cpv, sem.at[0])
    load_cp.start()
    load_rb = pltpu.make_async_copy(rb, rbv, sem.at[1])
    load_rb.start()
    highest = lax.Precision.HIGHEST

    work_a, work_r = [], []
    for i in range(4):
        rs = r_ref[pl.ds(4 * i, 4)].reshape(64, 128)
        middle = lax.dot_general(rs, g_ref[i], NN, precision=highest, preferred_element_type=F32)
        a = lax.dot_general(middle, rs, NT, precision=highest, preferred_element_type=F32)
        work_a.append([a[8 * b:8 * b + 8] for b in range(8)])
        work_r.append([rs[8 * b:8 * b + 8] for b in range(8)])

    sub = lax.broadcasted_iota(jnp.int32, (8, 128), 0)
    for step in range(16):
        b, o = divmod(4 * step, 8)
        for i in range(4):
            a, rr = work_a[i], work_r[i]
            cols = [
                [jnp.broadcast_to(a[n][:, 4 * step + p:4 * step + p + 1], (8, 128)) for n in range(b, 8)]
                for p in range(4)
            ]
            ra = [a[b][o + p:o + p + 1] for p in range(4)]
            rw = [rr[b][o + p:o + p + 1] for p in range(4)]
            mult, ua, ur = [], [], []
            for p in range(4):
                col, va, vr = cols[p], ra[p], rw[p]
                for q in range(p):
                    l = mult[q][0][o + p:o + p + 1]
                    col = [cc - mm * l for cc, mm in zip(col, mult[q])]
                    va = va - l[:, :64] * ua[q]
                    vr = vr - l * ur[q]
                inv = lax.rsqrt(col[0][o + p:o + p + 1])
                mult.append([cc * inv for cc in col])
                ua.append(va * inv[:, :64])
                ur.append(vr * inv)
            below = sub >= o + 4
            for n in range(b, 8):
                if n == b and o == 4:
                    continue
                da = sum(mult[p][n - b][:, :64] * ua[p] for p in range(4))
                dr = sum(mult[p][n - b] * ur[p] for p in range(4))
                if n == b:
                    da = jnp.where(below[:, :64], da, 0.0)
                    dr = jnp.where(below, dr, 0.0)
                a[n] = a[n] - da
                rr[n] = rr[n] - dr
            fin = rr[b]
            for p in range(4):
                fin = jnp.where(sub == o + p, ur[p], fin)
            rr[b] = fin

    load_rb.wait()
    for i in range(4):
        coeff = jnp.concatenate(work_r[i], axis=0)
        hi, lo = split_hi_lo(coeff)
        basis = rbv[i]
        nb[i] = (
            lax.dot_general(hi, basis, NN, preferred_element_type=F32)
            + lax.dot_general(lo, basis, NN, preferred_element_type=F32)
        )
        p = lax.dot_general(coeff, g_ref[i], NN, precision=highest, preferred_element_type=F32)
        hi, lo = split_hi_lo(p)
        proj[i] = jnp.concatenate([hi, lo], axis=0)

    load_cp.wait()
    first = lax.broadcasted_iota(jnp.int32, (64, 128), 1) < 64
    outs = [pltpu.make_async_copy(ncv.at[pl.ds(8 * n, 8)], nc.at[pl.ds(8 * n, 8)], out_sem.at[n]) for n in range(8)]
    for n in range(8):
        for t in range(8 * n, 8 * n + 8):
            row = rows_s[t]
            coupling = cpv[t].astype(F32)
            zero = jnp.zeros_like(coupling)
            pair = jnp.concatenate(
                [jnp.where(first, coupling, zero), jnp.where(first, zero, coupling)], axis=0
            ).astype(BF16)
            both = lax.dot_general(proj[jnp.minimum(row, 3)], pair, NN, preferred_element_type=F32)
            live = jnp.where(row < 4, 1.0, 0.0)
            ncv[t] = (both[:64] + both[64:]) * live
        outs[n].start()
    for copy in outs:
        copy.wait()


def back(tile_rows, r_side, gram, rb, cp):
    any_space = pl.BlockSpec(memory_space=pl.ANY)
    vmem = pl.BlockSpec(memory_space=pltpu.VMEM)
    return pl.pallas_call(
        back_kernel,
        out_shape=(
            jax.ShapeDtypeStruct((4, 64, 128), F32),
            jax.ShapeDtypeStruct((64, 64, 128), F32),
        ),
        in_specs=[pl.BlockSpec(memory_space=pltpu.SMEM), vmem, vmem, any_space, any_space],
        out_specs=(vmem, any_space),
        scratch_shapes=[
            pltpu.VMEM((64, 64, 128), BF16),
            pltpu.VMEM((4, 128, 128), BF16),
            pltpu.VMEM((64, 64, 128), F32),
            pltpu.VMEM((4, 128, 128), BF16),
            pltpu.SemaphoreType.DMA((2,)),
            pltpu.SemaphoreType.DMA((8,)),
        ],
        compiler_params=pltpu.CompilerParams(vmem_limit_bytes=60 * 1024 * 1024),
    )(tile_rows, r_side, gram, rb, cp)


def local(row_bases, col_bases, test_matrix, couplings, tile_rows, tile_cols):
    r_side, gram = front(
        col_bases, test_matrix, couplings, row_bases, tile_cols.reshape(1, 64), tile_rows.reshape(1, 64)
    )
    return back(tile_rows, r_side, gram, row_bases, couplings)


def solution(mesh):
    in_specs = (
        P("rows", None, "cols"),
        P("cols", None, "rows"),
        P("cols", None, "rows"),
        P(("rows", "cols"), None, None),
        P(("rows", "cols")),
        P(("rows", "cols")),
    )
    out_specs = (P("rows", None, "cols"), P(("rows", "cols"), None, None))
    return jax.shard_map(local, mesh=mesh, in_specs=in_specs, out_specs=out_specs, check_vma=False)
```

```python
import functools
import math

import jax
import jax.numpy as jnp
from jax import lax
from jax.experimental import pallas as pl
from jax.experimental.pallas import tpu as pltpu
from jax.sharding import PartitionSpec as P

MESH = pl.DeviceIdType.MESH
F32 = jnp.float32
BF16 = jnp.bfloat16
LEAF = 2048
SCALE = 1.0 / math.sqrt(LEAF)
CB = 48
HALF = 24
CH = 6
HC = 3
NCOL = 16
NT = (((1,), (1,)), ((), ()))
NN = (((1,), (0,)), ((), ()))
OFFSETS = sorted(
    [(dy, dx) for dy in range(4) for dx in range(4) if (dy, dx) != (0, 0)],
    key=lambda o: -min(o[0], 4 - o[0]) - min(o[1], 4 - o[1]),
)


STEPS = 32400.0


def split_hi_lo(value):
    hi = value.astype(BF16)
    return hi, (value - hi.astype(F32)).astype(BF16)


def code(value):
    head = value.astype(BF16)
    base = head.astype(F32)
    rest = (value - base) * pl.reciprocal(jnp.maximum(jnp.abs(base), 1e-30), approx=True)
    steps = jnp.floor(rest * STEPS + 0.5)
    return head, (steps[:32] * 256.0 + steps[32:]).astype(jnp.int32).astype(jnp.int16)


def rest_of(head, word):
    word = word.astype(jnp.int32)
    top = (word + 128) >> 8
    steps = jnp.concatenate([top, word - top * 256], axis=0).astype(F32)
    return jnp.abs(head.astype(F32)) * (steps * (1.0 / STEPS))


def front_kernel(
    cb, tm, cp, rb, tcols, trows, out_r, out_g,
    cbv, tmv, rbv, part, own, prx, zsh, zsw, zrh, zrw, skw, skb, cpl, pairs, idxv, idxs,
    gpart, grx, gall, rpart, rrx, rall,
    ld_sem, misc_sem, pc_send, pc_recv, zs_send, zs_recv, ag_send, ag_recv, fw_send, fw_recv,
    cp_send, cp_recv, ix_send, ix_recv, g1_send, g1_recv, g2_send, g2_recv,
    r1_send, r1_recv, r2_send, r2_recv,
):
    r = lax.axis_index("rows")
    k = lax.axis_index("cols")
    z, h = lax.div(r, 2), lax.rem(r, 2)
    y, x = lax.div(k, 4), lax.rem(k, 4)
    partner = (r + 1 - 2 * h, k)
    along = {q: (lax.rem(z + q, 4) * 2 + h, k) for q in (1, 2, 3)}
    peers = [lax.rem(y + dy, 4) * 4 + lax.rem(x + dx, 4) for dy, dx in OFFSETS]

    def piece(s, q):
        return lax.rem(z + q, 4) * CH + s * HC

    order = [(s, q) for s in (0, 1) for q in (2, 1, 3, 0)]
    loads = {}
    for n, half in enumerate((1 - h, h)):
        for m, (s, q) in enumerate(order):
            at = pl.ds(half * HALF + piece(s, q), HC)
            a = pltpu.make_async_copy(cb.at[at], cbv.at[at], ld_sem.at[0, n * 8 + m])
            b = pltpu.make_async_copy(tm.at[at], tmv.at[at], ld_sem.at[1, n * 8 + m])
            a.start()
            b.start()
            loads[n, s, q] = (a, b)
    load_rb = pltpu.make_async_copy(rb, rbv, misc_sem.at[0])
    load_rb.start()
    own_cp = pltpu.make_async_copy(cp.at[pl.ds(4 * k, 4)], cpl.at[k], misc_sem.at[1])
    own_cp.start()

    barrier = pltpu.get_barrier_semaphore()
    for device in [partner, along[1], along[2], along[3]] + [(r, c) for c in peers]:
        pl.semaphore_signal(barrier, inc=1, device_id=device, device_id_type=MESH)

    def sketch(n, s, q, dst):
        for load in loads[n, s, q]:
            load.wait()
        half = (1 - h) if n == 0 else h
        base = half * HALF + piece(s, q)
        for u in range(HC):
            dst[piece(s, q) + u] = (
                lax.dot_general(tmv[base + u], cbv[base + u], NT, preferred_element_type=F32) * SCALE
            )

    def remote(src, dst, send, recv, device):
        return pltpu.make_async_remote_copy(
            src_ref=src, dst_ref=dst, send_sem=send, recv_sem=recv, device_id=device, device_id_type=MESH
        )

    started = []

    def go(copy):
        copy.start()
        started.append(copy)
        return copy

    for s, q in order:
        sketch(0, s, q, part)
    idxv[k] = jnp.concatenate([tcols[...], trows[...]], axis=1)
    pl.semaphore_wait(barrier, 4 + len(OFFSETS))
    to_partner = {}
    for m, (s, q) in enumerate(order):
        at = pl.ds(piece(s, q), HC)
        to_partner[s, q] = go(remote(part.at[at], prx.at[at], pc_send.at[m], pc_recv.at[m], partner))
    labels = [
        go(remote(idxv.at[k], idxv.at[k], ix_send.at[n], ix_recv.at[n], (r, c)))
        for n, c in enumerate(peers)
    ]
    moves = [
        go(remote(cp.at[pl.ds(4 * c, 4)], cpl.at[k], cp_send.at[n], cp_recv.at[n], (r, c)))
        for n, c in enumerate(peers)
    ]

    scatter = {}
    for s, q in order:
        sketch(1, s, q, own)
        to_partner[s, q].wait_recv()
        at = piece(s, q)
        if not q:
            own[pl.ds(at, HC)] = own[pl.ds(at, HC)] + prx[pl.ds(at, HC)]
            continue
        n = 3 * s + q - 1
        for u in range(HC):
            zsh[n, u], zsw[n, u] = code(own[at + u] + prx[at + u])
        scatter[s, q] = (
            go(remote(zsh.at[n], zrh.at[n], zs_send.at[2 * n], zs_recv.at[2 * n], along[q])),
            go(remote(zsw.at[n], zrw.at[n], zs_send.at[2 * n + 1], zs_recv.at[2 * n + 1], along[q])),
        )


    load_rb.wait()
    for i in range(4):
        gpart[:, pl.ds(i * 128, 128)] = lax.dot_general(rbv[i], rbv[i], NT, preferred_element_type=F32) * (1.0 / LEAF)
    gram1 = [
        go(remote(gpart.at[pl.ds(8 * c, 8)], grx.at[n], g1_send.at[n], g1_recv.at[n], (r, c)))
        for n, c in enumerate(peers)
    ]

    def spread(start, send, recv, n, device):
        heads = skb.at[pl.ds(start, HC), pl.ds(0, 64)]
        words = skw.at[pl.ds(start, HC)]
        return (
            go(remote(heads, heads, send.at[2 * n], recv.at[2 * n], device)),
            go(remote(words, words, send.at[2 * n + 1], recv.at[2 * n + 1], device)),
        )

    def arrived(copies):
        for copy in copies:
            copy.wait_recv()

    def rests(start):
        for u in range(HC):
            skb[start + u, 64:] = rest_of(skb[start + u, :64], skw[start + u]).astype(BF16)

    gather, forwarded = {}, []
    for s in (0, 1):
        for q in (1, 2, 3):
            arrived(scatter[s, q])
        mine = h * HALF + piece(s, 0)
        for u in range(HC):
            total = own[piece(s, 0) + u]
            for n in range(3 * s, 3 * s + 3):
                head = zrh[n, u]
                total = total + (head.astype(F32) + rest_of(head, zrw[n, u]))
            skb[mine + u, :64], skw[mine + u] = code(total)
        for q in (2, 1, 3):
            gather[s, q] = spread(mine, ag_send, ag_recv, 3 * s + q - 1, along[q])
        forwarded.append((s, 0, spread(mine, fw_send, fw_recv, 4 * s, partner)))
        rests(mine)

    for s in (0, 1):
        for q in (1, 3, 2):
            arrived(gather[s, q])
            start = h * HALF + piece(s, 4 - q)
            forwarded.append((s, 4 - q, spread(start, fw_send, fw_recv, 4 * s + q, partner)))
            rests(start)

    own_cp.wait()
    for copy in labels:
        copy.wait_recv()
    for copy in moves:
        copy.wait_recv()
    to_scalars = pltpu.make_async_copy(idxv, idxs, misc_sem.at[2])
    to_scalars.start()
    first = lax.broadcasted_iota(jnp.int32, (64, 128), 1) < 64

    @pl.loop(0, NCOL)
    def _(c):
        for s in range(4):
            coupling = cpl[c, s].astype(F32)
            zero = jnp.zeros_like(coupling)
            pairs[4 * c + s] = jnp.concatenate(
                [jnp.where(first, coupling, zero), jnp.where(first, zero, coupling)], axis=0
            ).astype(BF16)

    to_scalars.wait()
    for s, q, copies in forwarded:
        arrived(copies)
        rests((1 - h) * HALF + piece(s, q))
    for copy in gram1:
        copy.wait_recv()
    total = gpart[pl.ds(pl.multiple_of(8 * k, 8), 8)]
    for n in range(len(OFFSETS)):
        total = total + grx[n]
    gall[k] = total
    gram2 = [
        go(remote(gall.at[k], gall.at[k], g2_send.at[n], g2_recv.at[n], (r, c)))
        for n, c in enumerate(peers)
    ]

    def tiles(n, carry):
        sums = list(carry)
        for m in range(8):
            c, s = 2 * n + m // 4, m % 4
            j = jnp.clip(idxs[c, 0, 4 * k + s] - CB * k, 0, CB - 1)
            row = idxs[c, 0, 64 + 4 * k + s]
            both = lax.dot_general(skb[j], pairs[4 * c + s], NT, preferred_element_type=F32)
            term = both[:64] + both[64:]
            for i in range(4):
                sums[i] = sums[i] + jnp.where(row == i, 1.0, 0.0) * term
        return tuple(sums)

    sums = lax.fori_loop(0, NCOL // 2, tiles, (jnp.zeros((64, 128), F32),) * 4)
    for i in range(4):
        rpart[pl.ds(4 * i, 4)] = sums[i].reshape(4, 16, 128)

    row1 = [
        go(remote(rpart.at[c], rrx.at[n], r1_send.at[n], r1_recv.at[n], (r, c)))
        for n, c in enumerate(peers)
    ]
    for copy in gram2:
        copy.wait_recv()
    for c in range(NCOL):
        for i in range(4):
            out_g[i, pl.ds(8 * c, 8)] = gall[c, :, pl.ds(128 * i, 128)]
    for copy in row1:
        copy.wait_recv()
    total = rpart[k]
    for n in range(len(OFFSETS)):
        total = total + rrx[n]
    rall[k] = total
    row2 = [
        go(remote(rall.at[k], rall.at[k], r2_send.at[n], r2_recv.at[n], (r, c)))
        for n, c in enumerate(peers)
    ]
    for copy in row2:
        copy.wait_recv()
    out_r[...] = rall[...]
    for copy in started:
        copy.wait_send()


def front(cb, tm, cp, rb, tcols, trows):
    any_space = pl.BlockSpec(memory_space=pl.ANY)
    vmem = pl.BlockSpec(memory_space=pltpu.VMEM)
    dma = pltpu.SemaphoreType.DMA
    peers = len(OFFSETS)
    return pl.pallas_call(
        front_kernel,
        out_shape=(
            jax.ShapeDtypeStruct((NCOL, 16, 128), F32),
            jax.ShapeDtypeStruct((4, 128, 128), F32),
        ),
        in_specs=[any_space] * 4 + [vmem] * 2,
        out_specs=(vmem, vmem),
        scratch_shapes=[
            pltpu.VMEM((CB, 128, 256), BF16),
            pltpu.VMEM((CB, 64, 256), BF16),
            pltpu.VMEM((4, 128, 128), BF16),
            pltpu.VMEM((HALF, 64, 128), F32),
            pltpu.VMEM((HALF, 64, 128), F32),
            pltpu.VMEM((HALF, 64, 128), F32),
            pltpu.VMEM((6, HC, 64, 128), BF16),
            pltpu.VMEM((6, HC, 32, 128), jnp.int16),
            pltpu.VMEM((6, HC, 64, 128), BF16),
            pltpu.VMEM((6, HC, 32, 128), jnp.int16),
            pltpu.VMEM((CB, 32, 128), jnp.int16),
            pltpu.VMEM((CB, 128, 128), BF16),
            pltpu.VMEM((NCOL, 4, 64, 128), BF16),
            pltpu.VMEM((64, 128, 128), BF16),
            pltpu.VMEM((NCOL, 1, 128), jnp.int32),
            pltpu.SMEM((NCOL, 1, 128), jnp.int32),
            pltpu.VMEM((128, 512), F32),
            pltpu.VMEM((peers, 8, 512), F32),
            pltpu.VMEM((NCOL, 8, 512), F32),
            pltpu.VMEM((NCOL, 16, 128), F32),
            pltpu.VMEM((peers, 16, 128), F32),
            pltpu.VMEM((NCOL, 16, 128), F32),
            dma((2, 16)), dma((3,)),
            dma((8,)), dma((8,)), dma((12,)), dma((12,)), dma((12,)), dma((12,)), dma((16,)), dma((16,)),
        ] + [dma((peers,))] * 12,
        compiler_params=pltpu.CompilerParams(
            collective_id=0, has_side_effects=True, vmem_limit_bytes=60 * 1024 * 1024
        ),
    )(cb, tm, cp, rb, tcols, trows)


def back_kernel(rows_s, r_ref, g_ref, rb, cp, nb, nc, cpv, rbv, ncv, proj, sem, out_sem):
    load_cp = pltpu.make_async_copy(cp, cpv, sem.at[0])
    load_cp.start()
    load_rb = pltpu.make_async_copy(rb, rbv, sem.at[1])
    load_rb.start()
    highest = lax.Precision.HIGHEST

    work_a, work_r = [], []
    for i in range(4):
        rs = r_ref[pl.ds(4 * i, 4)].reshape(64, 128)
        middle = lax.dot_general(rs, g_ref[i], NN, precision=highest, preferred_element_type=F32)
        a = lax.dot_general(middle, rs, NT, precision=highest, preferred_element_type=F32)
        work_a.append([a[8 * b:8 * b + 8] for b in range(8)])
        work_r.append([rs[8 * b:8 * b + 8] for b in range(8)])

    sub = lax.broadcasted_iota(jnp.int32, (8, 128), 0)
    for step in range(16):
        b, o = divmod(4 * step, 8)
        for i in range(4):
            a, rr = work_a[i], work_r[i]
            cols = [
                [jnp.broadcast_to(a[n][:, 4 * step + p:4 * step + p + 1], (8, 128)) for n in range(b, 8)]
                for p in range(4)
            ]
            ra = [a[b][o + p:o + p + 1] for p in range(4)]
            rw = [rr[b][o + p:o + p + 1] for p in range(4)]
            mult, ua, ur = [], [], []
            for p in range(4):
                col, va, vr = cols[p], ra[p], rw[p]
                for q in range(p):
                    l = mult[q][0][o + p:o + p + 1]
                    col = [cc - mm * l for cc, mm in zip(col, mult[q])]
                    va = va - l[:, :64] * ua[q]
                    vr = vr - l * ur[q]
                inv = lax.rsqrt(col[0][o + p:o + p + 1])
                mult.append([cc * inv for cc in col])
                ua.append(va * inv[:, :64])
                ur.append(vr * inv)
            below = sub >= o + 4
            for n in range(b, 8):
                if n == b and o == 4:
                    continue
                da = sum(mult[p][n - b][:, :64] * ua[p] for p in range(4))
                dr = sum(mult[p][n - b] * ur[p] for p in range(4))
                if n == b:
                    da = jnp.where(below[:, :64], da, 0.0)
                    dr = jnp.where(below, dr, 0.0)
                a[n] = a[n] - da
                rr[n] = rr[n] - dr
            fin = rr[b]
            for p in range(4):
                fin = jnp.where(sub == o + p, ur[p], fin)
            rr[b] = fin

    load_rb.wait()
    for i in range(4):
        coeff = jnp.concatenate(work_r[i], axis=0)
        hi, lo = split_hi_lo(coeff)
        basis = rbv[i]
        nb[i] = (
            lax.dot_general(hi, basis, NN, preferred_element_type=F32)
            + lax.dot_general(lo, basis, NN, preferred_element_type=F32)
        )
        p = lax.dot_general(coeff, g_ref[i], NN, precision=highest, preferred_element_type=F32)
        hi, lo = split_hi_lo(p)
        proj[i] = jnp.concatenate([hi, lo], axis=0)

    load_cp.wait()
    first = lax.broadcasted_iota(jnp.int32, (64, 128), 1) < 64
    outs = [pltpu.make_async_copy(ncv.at[pl.ds(8 * n, 8)], nc.at[pl.ds(8 * n, 8)], out_sem.at[n]) for n in range(8)]
    for n in range(8):
        for t in range(8 * n, 8 * n + 8):
            row = rows_s[t]
            coupling = cpv[t].astype(F32)
            zero = jnp.zeros_like(coupling)
            pair = jnp.concatenate(
                [jnp.where(first, coupling, zero), jnp.where(first, zero, coupling)], axis=0
            ).astype(BF16)
            both = lax.dot_general(proj[jnp.minimum(row, 3)], pair, NN, preferred_element_type=F32)
            live = jnp.where(row < 4, 1.0, 0.0)
            ncv[t] = (both[:64] + both[64:]) * live
        outs[n].start()
    for copy in outs:
        copy.wait()


def back(tile_rows, r_side, gram, rb, cp):
    any_space = pl.BlockSpec(memory_space=pl.ANY)
    vmem = pl.BlockSpec(memory_space=pltpu.VMEM)
    return pl.pallas_call(
        back_kernel,
        out_shape=(
            jax.ShapeDtypeStruct((4, 64, 128), F32),
            jax.ShapeDtypeStruct((64, 64, 128), F32),
        ),
        in_specs=[pl.BlockSpec(memory_space=pltpu.SMEM), vmem, vmem, any_space, any_space],
        out_specs=(vmem, any_space),
        scratch_shapes=[
            pltpu.VMEM((64, 64, 128), BF16),
            pltpu.VMEM((4, 128, 128), BF16),
            pltpu.VMEM((64, 64, 128), F32),
            pltpu.VMEM((4, 128, 128), BF16),
            pltpu.SemaphoreType.DMA((2,)),
            pltpu.SemaphoreType.DMA((8,)),
        ],
        compiler_params=pltpu.CompilerParams(vmem_limit_bytes=60 * 1024 * 1024),
    )(tile_rows, r_side, gram, rb, cp)


def local(row_bases, col_bases, test_matrix, couplings, tile_rows, tile_cols):
    r_side, gram = front(
        col_bases, test_matrix, couplings, row_bases, tile_cols.reshape(1, 64), tile_rows.reshape(1, 64)
    )
    return back(tile_rows, r_side, gram, row_bases, couplings)


def solution(mesh):
    in_specs = (
        P("rows", None, "cols"),
        P("cols", None, "rows"),
        P("cols", None, "rows"),
        P(("rows", "cols"), None, None),
        P(("rows", "cols")),
        P(("rows", "cols")),
    )
    out_specs = (P("rows", None, "cols"), P(("rows", "cols"), None, None))
    return jax.shard_map(local, mesh=mesh, in_specs=in_specs, out_specs=out_specs, check_vma=False)
```

```python
import functools
import math

import jax
import jax.numpy as jnp
from jax import lax
from jax.experimental import pallas as pl
from jax.experimental.pallas import tpu as pltpu
from jax.sharding import PartitionSpec as P

MESH = pl.DeviceIdType.MESH
F32 = jnp.float32
BF16 = jnp.bfloat16
LEAF = 2048
SCALE = 1.0 / math.sqrt(LEAF)
CB = 48
HALF = 24
CH = 6
SUBS = 2
HC = CH // SUBS
NCOL = 16
STEP = 64
NT = (((1,), (1,)), ((), ()))
NN = (((1,), (0,)), ((), ()))
OFFSETS = sorted(
    [(dy, dx) for dy in range(4) for dx in range(4) if (dy, dx) != (0, 0)],
    key=lambda o: -min(o[0], 4 - o[0]) - min(o[1], 4 - o[1]),
)


STEPS = 32400.0


def split_hi_lo(value):
    hi = value.astype(BF16)
    return hi, (value - hi.astype(F32)).astype(BF16)


def code(value):
    head = value.astype(BF16)
    base = head.astype(F32)
    rest = (value - base) * pl.reciprocal(jnp.maximum(jnp.abs(base), 1e-30), approx=True)
    steps = jnp.floor(rest * STEPS + 0.5)
    return head, (steps[:32] * 256.0 + steps[32:]).astype(jnp.int32).astype(jnp.int16)


def rest_of(head, word):
    word = word.astype(jnp.int32)
    top = (word + 128) >> 8
    steps = jnp.concatenate([top, word - top * 256], axis=0).astype(F32)
    return jnp.abs(head.astype(F32)) * (steps * (1.0 / STEPS))


def front_kernel(
    cb, tm, cp, rb, tcols, trows, out_r, out_g,
    cbv, tmv, rbv, part, own, prx, zsh, zsw, zrh, zrw, skw, skb, cpl, pairs, idxv, idxs,
    gpart, grx, gall, rpart, rrx, rall,
    ld_sem, misc_sem, pc_send, pc_recv, zs_send, zs_recv, ag_send, ag_recv, fw_send, fw_recv,
    cp_send, cp_recv, ix_send, ix_recv, g1_send, g1_recv, g2_send, g2_recv,
    r1_send, r1_recv, r2_send, r2_recv,
):
    r = lax.axis_index("rows")
    k = lax.axis_index("cols")
    z, h = lax.div(r, 2), lax.rem(r, 2)
    y, x = lax.div(k, 4), lax.rem(k, 4)
    partner = (r + 1 - 2 * h, k)
    along = {q: (lax.rem(z + q, 4) * 2 + h, k) for q in (1, 2, 3)}
    peers = [lax.rem(y + dy, 4) * 4 + lax.rem(x + dx, 4) for dy, dx in OFFSETS]

    def piece(s, q):
        return lax.rem(z + q, 4) * CH + s * HC

    order = [(s, q) for s in range(SUBS) for q in (2, 1, 3, 0)]
    loads = {}
    for n, half in enumerate((1 - h, h)):
        for m, (s, q) in enumerate(order):
            at = pl.ds(half * HALF + piece(s, q), HC)
            a = pltpu.make_async_copy(cb.at[at], cbv.at[at], ld_sem.at[0, 4 * SUBS * n + m])
            b = pltpu.make_async_copy(tm.at[at], tmv.at[at], ld_sem.at[1, 4 * SUBS * n + m])
            a.start()
            b.start()
            loads[n, s, q] = (a, b)
    load_rb = pltpu.make_async_copy(rb, rbv, misc_sem.at[0])
    load_rb.start()
    own_cp = pltpu.make_async_copy(cp.at[pl.ds(4 * k, 4)], cpl.at[k], misc_sem.at[1])
    own_cp.start()

    barrier = pltpu.get_barrier_semaphore()
    for device in [partner, along[1], along[2], along[3]] + [(r, c) for c in peers]:
        pl.semaphore_signal(barrier, inc=1, device_id=device, device_id_type=MESH)

    def sketch(n, s, q, dst):
        for load in loads[n, s, q]:
            load.wait()
        half = (1 - h) if n == 0 else h
        base = half * HALF + piece(s, q)
        for u in range(HC):
            dst[piece(s, q) + u] = (
                lax.dot_general(tmv[base + u], cbv[base + u], NT, preferred_element_type=F32) * SCALE
            )

    def remote(src, dst, send, recv, device):
        return pltpu.make_async_remote_copy(
            src_ref=src, dst_ref=dst, send_sem=send, recv_sem=recv, device_id=device, device_id_type=MESH
        )

    started = []

    def go(copy):
        copy.start()
        started.append(copy)
        return copy

    for s, q in order:
        sketch(0, s, q, part)
    idxv[k] = jnp.concatenate([tcols[...], trows[...]], axis=1)
    load_rb.wait()
    for i in range(4):
        gpart[:, pl.ds(i * 128, 128)] = lax.dot_general(rbv[i], rbv[i], NT, preferred_element_type=F32) * (1.0 / LEAF)
    pl.semaphore_wait(barrier, 4 + len(OFFSETS))
    to_partner = {}
    for m, (s, q) in enumerate(order):
        at = pl.ds(piece(s, q), HC)
        to_partner[s, q] = go(remote(part.at[at], prx.at[at], pc_send.at[m], pc_recv.at[m], partner))
    labels = [
        go(remote(idxv.at[k], idxv.at[k], ix_send.at[n], ix_recv.at[n], (r, c)))
        for n, c in enumerate(peers)
    ]
    gram1 = [
        go(remote(gpart.at[pl.ds(8 * c, 8)], grx.at[n], g1_send.at[n], g1_recv.at[n], (r, c)))
        for n, c in enumerate(peers)
    ]
    moves = [
        go(remote(cp.at[pl.ds(4 * c, 4)], cpl.at[k], cp_send.at[n], cp_recv.at[n], (r, c)))
        for n, c in enumerate(peers)
    ]

    scatter = {}
    for s, q in order:
        sketch(1, s, q, own)
        to_partner[s, q].wait_recv()
        at = piece(s, q)
        if not q:
            own[pl.ds(at, HC)] = own[pl.ds(at, HC)] + prx[pl.ds(at, HC)]
            continue
        n = 3 * s + q - 1
        for u in range(HC):
            zsh[n, u], zsw[n, u] = code(own[at + u] + prx[at + u])
        scatter[s, q] = (
            go(remote(zsh.at[n], zrh.at[n], zs_send.at[2 * n], zs_recv.at[2 * n], along[q])),
            go(remote(zsw.at[n], zrw.at[n], zs_send.at[2 * n + 1], zs_recv.at[2 * n + 1], along[q])),
        )


    def spread(start, send, recv, n, device):
        heads = skb.at[pl.ds(start, HC), pl.ds(0, 64)]
        words = skw.at[pl.ds(start, HC)]
        return (
            go(remote(heads, heads, send.at[2 * n], recv.at[2 * n], device)),
            go(remote(words, words, send.at[2 * n + 1], recv.at[2 * n + 1], device)),
        )

    def arrived(copies):
        for copy in copies:
            copy.wait_recv()

    def rests(start):
        for u in range(HC):
            skb[start + u, 64:] = rest_of(skb[start + u, :64], skw[start + u]).astype(BF16)

    gather, forwarded = {}, []
    for s in range(SUBS):
        for q in (1, 2, 3):
            arrived(scatter[s, q])
        mine = h * HALF + piece(s, 0)
        for u in range(HC):
            total = own[piece(s, 0) + u]
            for n in range(3 * s, 3 * s + 3):
                head = zrh[n, u]
                total = total + (head.astype(F32) + rest_of(head, zrw[n, u]))
            skb[mine + u, :64], skw[mine + u] = code(total)
        for q in (2, 1, 3):
            gather[s, q] = spread(mine, ag_send, ag_recv, 3 * s + q - 1, along[q])
        forwarded.append((s, 0, spread(mine, fw_send, fw_recv, 4 * s, partner)))
        rests(mine)
    for copy in gram1:
        copy.wait_recv()
    total = gpart[pl.ds(pl.multiple_of(8 * k, 8), 8)]
    for n in range(len(OFFSETS)):
        total = total + grx[n]
    gall[k] = total
    gram2 = [
        go(remote(gall.at[k], gall.at[k], g2_send.at[n], g2_recv.at[n], (r, c)))
        for n, c in enumerate(peers)
    ]

    for s in range(SUBS):
        for q in (1, 3, 2):
            arrived(gather[s, q])
            start = h * HALF + piece(s, 4 - q)
            forwarded.append((s, 4 - q, spread(start, fw_send, fw_recv, 4 * s + q, partner)))
            rests(start)

    own_cp.wait()
    for copy in labels:
        copy.wait_recv()
    for copy in moves:
        copy.wait_recv()
    to_scalars = pltpu.make_async_copy(idxv, idxs, misc_sem.at[2])
    to_scalars.start()
    first = lax.broadcasted_iota(jnp.int32, (64, 128), 1) < 64

    @pl.loop(0, NCOL)
    def _(c):
        for s in range(4):
            coupling = cpl[c, s].astype(F32)
            zero = jnp.zeros_like(coupling)
            pairs[4 * c + s] = jnp.concatenate(
                [jnp.where(first, coupling, zero), jnp.where(first, zero, coupling)], axis=0
            ).astype(BF16)

    to_scalars.wait()
    for s, q, copies in forwarded:
        arrived(copies)
        rests((1 - h) * HALF + piece(s, q))

    def tiles(n, carry):
        sums = list(carry)
        for m in range(STEP):
            c, s = STEP // 4 * n + m // 4, m % 4
            j = jnp.clip(idxs[c, 0, 4 * k + s] - CB * k, 0, CB - 1)
            row = idxs[c, 0, 64 + 4 * k + s]
            both = lax.dot_general(skb[j], pairs[4 * c + s], NT, preferred_element_type=F32)
            term = both[:64] + both[64:]
            for i in range(4):
                sums[i] = sums[i] + jnp.where(row == i, 1.0, 0.0) * term
        return tuple(sums)

    sums = lax.fori_loop(0, 64 // STEP, tiles, (jnp.zeros((64, 128), F32),) * 4)
    for i in range(4):
        rpart[pl.ds(4 * i, 4)] = sums[i].reshape(4, 16, 128)

    row1 = [
        go(remote(rpart.at[c], rrx.at[n], r1_send.at[n], r1_recv.at[n], (r, c)))
        for n, c in enumerate(peers)
    ]
    for copy in gram2:
        copy.wait_recv()
    for c in range(NCOL):
        for i in range(4):
            out_g[i, pl.ds(8 * c, 8)] = gall[c, :, pl.ds(128 * i, 128)]
    for copy in row1:
        copy.wait_recv()
    total = rpart[k]
    for n in range(len(OFFSETS)):
        total = total + rrx[n]
    rall[k] = total
    row2 = [
        go(remote(rall.at[k], rall.at[k], r2_send.at[n], r2_recv.at[n], (r, c)))
        for n, c in enumerate(peers)
    ]
    for copy in row2:
        copy.wait_recv()
    out_r[...] = rall[...]
    for copy in started:
        copy.wait_send()


def front(cb, tm, cp, rb, tcols, trows):
    any_space = pl.BlockSpec(memory_space=pl.ANY)
    vmem = pl.BlockSpec(memory_space=pltpu.VMEM)
    dma = pltpu.SemaphoreType.DMA
    peers = len(OFFSETS)
    return pl.pallas_call(
        front_kernel,
        out_shape=(
            pltpu.VMEM((NCOL, 16, 128), F32),
            pltpu.VMEM((4, 128, 128), F32),
        ),
        in_specs=[any_space] * 4 + [vmem] * 2,
        out_specs=(vmem, vmem),
        scratch_shapes=[
            pltpu.VMEM((CB, 128, 256), BF16),
            pltpu.VMEM((CB, 64, 256), BF16),
            pltpu.VMEM((4, 128, 128), BF16),
            pltpu.VMEM((HALF, 64, 128), F32),
            pltpu.VMEM((HALF, 64, 128), F32),
            pltpu.VMEM((HALF, 64, 128), F32),
            pltpu.VMEM((3 * SUBS, HC, 64, 128), BF16),
            pltpu.VMEM((3 * SUBS, HC, 32, 128), jnp.int16),
            pltpu.VMEM((3 * SUBS, HC, 64, 128), BF16),
            pltpu.VMEM((3 * SUBS, HC, 32, 128), jnp.int16),
            pltpu.VMEM((CB, 32, 128), jnp.int16),
            pltpu.VMEM((CB, 128, 128), BF16),
            pltpu.VMEM((NCOL, 4, 64, 128), BF16),
            pltpu.VMEM((64, 128, 128), BF16),
            pltpu.VMEM((NCOL, 1, 128), jnp.int32),
            pltpu.SMEM((NCOL, 1, 128), jnp.int32),
            pltpu.VMEM((128, 512), F32),
            pltpu.VMEM((peers, 8, 512), F32),
            pltpu.VMEM((NCOL, 8, 512), F32),
            pltpu.VMEM((NCOL, 16, 128), F32),
            pltpu.VMEM((peers, 16, 128), F32),
            pltpu.VMEM((NCOL, 16, 128), F32),
            dma((2, 8 * SUBS)), dma((3,)),
            dma((4 * SUBS,)), dma((4 * SUBS,)),
        ] + [dma((6 * SUBS,))] * 4 + [dma((8 * SUBS,))] * 2 + [dma((peers,))] * 12,
        compiler_params=pltpu.CompilerParams(
            collective_id=0, has_side_effects=True, vmem_limit_bytes=60 * 1024 * 1024
        ),
    )(cb, tm, cp, rb, tcols, trows)


def back_kernel(rows_s, r_ref, g_ref, rb, cp, nb, nc, cpv, rbv, ncv, proj, sem, out_sem):
    load_cp = pltpu.make_async_copy(cp, cpv, sem.at[0])
    load_cp.start()
    load_rb = pltpu.make_async_copy(rb, rbv, sem.at[1])
    load_rb.start()
    highest = lax.Precision.HIGHEST

    work_a, work_r = [], []
    for i in range(4):
        rs = r_ref[pl.ds(4 * i, 4)].reshape(64, 128)
        middle = lax.dot_general(rs, g_ref[i], NN, precision=highest, preferred_element_type=F32)
        a = lax.dot_general(middle, rs, NT, precision=highest, preferred_element_type=F32)
        work_a.append([a[8 * b:8 * b + 8] for b in range(8)])
        work_r.append([rs[8 * b:8 * b + 8] for b in range(8)])

    sub = lax.broadcasted_iota(jnp.int32, (8, 128), 0)
    for step in range(16):
        b, o = divmod(4 * step, 8)
        for i in range(4):
            a, rr = work_a[i], work_r[i]
            cols = [
                [jnp.broadcast_to(a[n][:, 4 * step + p:4 * step + p + 1], (8, 128)) for n in range(b, 8)]
                for p in range(4)
            ]
            ra = [a[b][o + p:o + p + 1] for p in range(4)]
            rw = [rr[b][o + p:o + p + 1] for p in range(4)]
            mult, ua, ur = [], [], []
            for p in range(4):
                col, va, vr = cols[p], ra[p], rw[p]
                for q in range(p):
                    l = mult[q][0][o + p:o + p + 1]
                    col = [cc - mm * l for cc, mm in zip(col, mult[q])]
                    va = va - l[:, :64] * ua[q]
                    vr = vr - l * ur[q]
                inv = lax.rsqrt(col[0][o + p:o + p + 1])
                mult.append([cc * inv for cc in col])
                ua.append(va * inv[:, :64])
                ur.append(vr * inv)
            below = sub >= o + 4
            for n in range(b, 8):
                if n == b and o == 4:
                    continue
                da = sum(mult[p][n - b][:, :64] * ua[p] for p in range(4))
                dr = sum(mult[p][n - b] * ur[p] for p in range(4))
                if n == b:
                    da = jnp.where(below[:, :64], da, 0.0)
                    dr = jnp.where(below, dr, 0.0)
                a[n] = a[n] - da
                rr[n] = rr[n] - dr
            fin = rr[b]
            for p in range(4):
                fin = jnp.where(sub == o + p, ur[p], fin)
            rr[b] = fin

    load_rb.wait()
    for i in range(4):
        coeff = jnp.concatenate(work_r[i], axis=0)
        hi, lo = split_hi_lo(coeff)
        basis = rbv[i]
        nb[i] = (
            lax.dot_general(hi, basis, NN, preferred_element_type=F32)
            + lax.dot_general(lo, basis, NN, preferred_element_type=F32)
        )
        p = lax.dot_general(coeff, g_ref[i], NN, precision=highest, preferred_element_type=F32)
        hi, lo = split_hi_lo(p)
        proj[i] = jnp.concatenate([hi, lo], axis=0)

    load_cp.wait()
    first = lax.broadcasted_iota(jnp.int32, (64, 128), 1) < 64
    outs = [pltpu.make_async_copy(ncv.at[pl.ds(8 * n, 8)], nc.at[pl.ds(8 * n, 8)], out_sem.at[n]) for n in range(8)]
    for n in range(8):
        for t in range(8 * n, 8 * n + 8):
            row = rows_s[t]
            coupling = cpv[t].astype(F32)
            zero = jnp.zeros_like(coupling)
            pair = jnp.concatenate(
                [jnp.where(first, coupling, zero), jnp.where(first, zero, coupling)], axis=0
            ).astype(BF16)
            both = lax.dot_general(proj[jnp.minimum(row, 3)], pair, NN, preferred_element_type=F32)
            live = jnp.where(row < 4, 1.0, 0.0)
            ncv[t] = (both[:64] + both[64:]) * live
        outs[n].start()
    for copy in outs:
        copy.wait()


def back(tile_rows, r_side, gram, rb, cp):
    any_space = pl.BlockSpec(memory_space=pl.ANY)
    vmem = pl.BlockSpec(memory_space=pltpu.VMEM)
    return pl.pallas_call(
        back_kernel,
        out_shape=(
            jax.ShapeDtypeStruct((4, 64, 128), F32),
            jax.ShapeDtypeStruct((64, 64, 128), F32),
        ),
        in_specs=[pl.BlockSpec(memory_space=pltpu.SMEM), vmem, vmem, any_space, any_space],
        out_specs=(vmem, any_space),
        scratch_shapes=[
            pltpu.VMEM((64, 64, 128), BF16),
            pltpu.VMEM((4, 128, 128), BF16),
            pltpu.VMEM((64, 64, 128), F32),
            pltpu.VMEM((4, 128, 128), BF16),
            pltpu.SemaphoreType.DMA((2,)),
            pltpu.SemaphoreType.DMA((8,)),
        ],
        compiler_params=pltpu.CompilerParams(vmem_limit_bytes=60 * 1024 * 1024),
    )(tile_rows, r_side, gram, rb, cp)


def local(row_bases, col_bases, test_matrix, couplings, tile_rows, tile_cols):
    r_side, gram = front(
        col_bases, test_matrix, couplings, row_bases, tile_cols.reshape(1, 64), tile_rows.reshape(1, 64)
    )
    r_side = pltpu.with_memory_space_constraint(r_side, pltpu.VMEM)
    gram = pltpu.with_memory_space_constraint(gram, pltpu.VMEM)
    return back(tile_rows, r_side, gram, row_bases, couplings)


def solution(mesh):
    in_specs = (
        P("rows", None, "cols"),
        P("cols", None, "rows"),
        P("cols", None, "rows"),
        P(("rows", "cols"), None, None),
        P(("rows", "cols")),
        P(("rows", "cols")),
    )
    out_specs = (P("rows", None, "cols"), P(("rows", "cols"), None, None))
    return jax.shard_map(local, mesh=mesh, in_specs=in_specs, out_specs=out_specs, check_vma=False)
```

```python
import functools
import math

import jax
import jax.numpy as jnp
from jax import lax
from jax.experimental import pallas as pl
from jax.experimental.pallas import tpu as pltpu
from jax.sharding import PartitionSpec as P

MESH = pl.DeviceIdType.MESH
F32 = jnp.float32
BF16 = jnp.bfloat16
LEAF = 2048
SCALE = 1.0 / math.sqrt(LEAF)
CB = 48
HALF = 24
CH = 6
SUBS = 2
HC = CH // SUBS
NCOL = 16
STEP = 64
PIVOTS = 8
NT = (((1,), (1,)), ((), ()))
NN = (((1,), (0,)), ((), ()))
OFFSETS = sorted(
    [(dy, dx) for dy in range(4) for dx in range(4) if (dy, dx) != (0, 0)],
    key=lambda o: -min(o[0], 4 - o[0]) - min(o[1], 4 - o[1]),
)


STEPS = 32400.0


def split_hi_lo(value):
    hi = value.astype(BF16)
    return hi, (value - hi.astype(F32)).astype(BF16)


def code(value):
    head = value.astype(BF16)
    base = head.astype(F32)
    rest = (value - base) * pl.reciprocal(jnp.maximum(jnp.abs(base), 1e-30), approx=True)
    steps = jnp.floor(rest * STEPS + 0.5)
    return head, (steps[:32] * 256.0 + steps[32:]).astype(jnp.int32).astype(jnp.int16)


def rest_of(head, word):
    word = word.astype(jnp.int32)
    top = (word + 128) >> 8
    steps = jnp.concatenate([top, word - top * 256], axis=0).astype(F32)
    return jnp.abs(head.astype(F32)) * (steps * (1.0 / STEPS))


def front_kernel(
    cb, tm, cp, rb, tcols, trows, out_r, out_g,
    cbv, tmv, rbv, part, own, prx, zsh, zsw, zrh, zrw, skw, skb, cpl, pairs, idxv, idxs,
    gpart, grx, gall, rpart, rrx, rall,
    ld_sem, misc_sem, pc_send, pc_recv, zs_send, zs_recv, ag_send, ag_recv, fw_send, fw_recv,
    cp_send, cp_recv, ix_send, ix_recv, g1_send, g1_recv, g2_send, g2_recv,
    r1_send, r1_recv, r2_send, r2_recv,
):
    r = lax.axis_index("rows")
    k = lax.axis_index("cols")
    z, h = lax.div(r, 2), lax.rem(r, 2)
    y, x = lax.div(k, 4), lax.rem(k, 4)
    partner = (r + 1 - 2 * h, k)
    along = {q: (lax.rem(z + q, 4) * 2 + h, k) for q in (1, 2, 3)}
    peers = [lax.rem(y + dy, 4) * 4 + lax.rem(x + dx, 4) for dy, dx in OFFSETS]

    def piece(s, q):
        return lax.rem(z + q, 4) * CH + s * HC

    order = [(s, q) for s in range(SUBS) for q in (2, 1, 3, 0)]
    loads = {}
    for n, half in enumerate((1 - h, h)):
        for m, (s, q) in enumerate(order):
            at = pl.ds(half * HALF + piece(s, q), HC)
            a = pltpu.make_async_copy(cb.at[at], cbv.at[at], ld_sem.at[0, 4 * SUBS * n + m])
            b = pltpu.make_async_copy(tm.at[at], tmv.at[at], ld_sem.at[1, 4 * SUBS * n + m])
            a.start()
            b.start()
            loads[n, s, q] = (a, b)
    load_rb = pltpu.make_async_copy(rb, rbv, misc_sem.at[0])
    load_rb.start()
    own_cp = pltpu.make_async_copy(cp.at[pl.ds(4 * k, 4)], cpl.at[k], misc_sem.at[1])
    own_cp.start()

    barrier = pltpu.get_barrier_semaphore()
    for device in [partner, along[1], along[2], along[3]] + [(r, c) for c in peers]:
        pl.semaphore_signal(barrier, inc=1, device_id=device, device_id_type=MESH)

    def sketch(n, s, q, dst):
        for load in loads[n, s, q]:
            load.wait()
        half = (1 - h) if n == 0 else h
        base = half * HALF + piece(s, q)
        for u in range(HC):
            dst[piece(s, q) + u] = (
                lax.dot_general(tmv[base + u], cbv[base + u], NT, preferred_element_type=F32) * SCALE
            )

    def remote(src, dst, send, recv, device):
        return pltpu.make_async_remote_copy(
            src_ref=src, dst_ref=dst, send_sem=send, recv_sem=recv, device_id=device, device_id_type=MESH
        )

    started = []

    def go(copy):
        copy.start()
        started.append(copy)
        return copy

    for s, q in order:
        sketch(0, s, q, part)
    idxv[k] = jnp.concatenate([tcols[...], trows[...]], axis=1)
    load_rb.wait()
    for i in range(4):
        gpart[:, pl.ds(i * 128, 128)] = lax.dot_general(rbv[i], rbv[i], NT, preferred_element_type=F32) * (1.0 / LEAF)
    pl.semaphore_wait(barrier, 4 + len(OFFSETS))
    to_partner = {}
    for m, (s, q) in enumerate(order):
        at = pl.ds(piece(s, q), HC)
        to_partner[s, q] = go(remote(part.at[at], prx.at[at], pc_send.at[m], pc_recv.at[m], partner))
    labels = [
        go(remote(idxv.at[k], idxv.at[k], ix_send.at[n], ix_recv.at[n], (r, c)))
        for n, c in enumerate(peers)
    ]
    gram1 = [
        go(remote(gpart.at[pl.ds(8 * c, 8)], grx.at[n], g1_send.at[n], g1_recv.at[n], (r, c)))
        for n, c in enumerate(peers)
    ]
    moves = [
        go(remote(cp.at[pl.ds(4 * c, 4)], cpl.at[k], cp_send.at[n], cp_recv.at[n], (r, c)))
        for n, c in enumerate(peers)
    ]

    scatter = {}
    for s, q in order:
        sketch(1, s, q, own)
        to_partner[s, q].wait_recv()
        at = piece(s, q)
        if not q:
            own[pl.ds(at, HC)] = own[pl.ds(at, HC)] + prx[pl.ds(at, HC)]
            continue
        n = 3 * s + q - 1
        for u in range(HC):
            zsh[n, u], zsw[n, u] = code(own[at + u] + prx[at + u])
        scatter[s, q] = (
            go(remote(zsh.at[n], zrh.at[n], zs_send.at[2 * n], zs_recv.at[2 * n], along[q])),
            go(remote(zsw.at[n], zrw.at[n], zs_send.at[2 * n + 1], zs_recv.at[2 * n + 1], along[q])),
        )


    def spread(start, send, recv, n, device):
        heads = skb.at[pl.ds(start, HC), pl.ds(0, 64)]
        words = skw.at[pl.ds(start, HC)]
        return (
            go(remote(heads, heads, send.at[2 * n], recv.at[2 * n], device)),
            go(remote(words, words, send.at[2 * n + 1], recv.at[2 * n + 1], device)),
        )

    def arrived(copies):
        for copy in copies:
            copy.wait_recv()

    def rests(start):
        for u in range(HC):
            skb[start + u, 64:] = rest_of(skb[start + u, :64], skw[start + u]).astype(BF16)

    gather, forwarded = {}, []
    for s in range(SUBS):
        for q in (1, 2, 3):
            arrived(scatter[s, q])
        mine = h * HALF + piece(s, 0)
        for u in range(HC):
            total = own[piece(s, 0) + u]
            for n in range(3 * s, 3 * s + 3):
                head = zrh[n, u]
                total = total + (head.astype(F32) + rest_of(head, zrw[n, u]))
            skb[mine + u, :64], skw[mine + u] = code(total)
        for q in (2, 1, 3):
            gather[s, q] = spread(mine, ag_send, ag_recv, 3 * s + q - 1, along[q])
        forwarded.append((s, 0, spread(mine, fw_send, fw_recv, 4 * s, partner)))
        rests(mine)
    for copy in gram1:
        copy.wait_recv()
    total = gpart[pl.ds(pl.multiple_of(8 * k, 8), 8)]
    for n in range(len(OFFSETS)):
        total = total + grx[n]
    gall[k] = total
    gram2 = [
        go(remote(gall.at[k], gall.at[k], g2_send.at[n], g2_recv.at[n], (r, c)))
        for n, c in enumerate(peers)
    ]

    for s in range(SUBS):
        for q in (1, 3, 2):
            arrived(gather[s, q])
            start = h * HALF + piece(s, 4 - q)
            forwarded.append((s, 4 - q, spread(start, fw_send, fw_recv, 4 * s + q, partner)))
            rests(start)

    own_cp.wait()
    for copy in labels:
        copy.wait_recv()
    for copy in moves:
        copy.wait_recv()
    to_scalars = pltpu.make_async_copy(idxv, idxs, misc_sem.at[2])
    to_scalars.start()
    first = lax.broadcasted_iota(jnp.int32, (64, 128), 1) < 64

    @pl.loop(0, NCOL)
    def _(c):
        for s in range(4):
            coupling = cpl[c, s].astype(F32)
            zero = jnp.zeros_like(coupling)
            pairs[4 * c + s] = jnp.concatenate(
                [jnp.where(first, coupling, zero), jnp.where(first, zero, coupling)], axis=0
            ).astype(BF16)

    to_scalars.wait()
    for s, q, copies in forwarded:
        arrived(copies)
        rests((1 - h) * HALF + piece(s, q))

    def tiles(n, carry):
        sums = list(carry)
        for m in range(STEP):
            c, s = STEP // 4 * n + m // 4, m % 4
            j = jnp.clip(idxs[c, 0, 4 * k + s] - CB * k, 0, CB - 1)
            row = idxs[c, 0, 64 + 4 * k + s]
            both = lax.dot_general(skb[j], pairs[4 * c + s], NT, preferred_element_type=F32)
            term = both[:64] + both[64:]
            for i in range(4):
                sums[i] = sums[i] + jnp.where(row == i, 1.0, 0.0) * term
        return tuple(sums)

    sums = lax.fori_loop(0, 64 // STEP, tiles, (jnp.zeros((64, 128), F32),) * 4)
    for i in range(4):
        rpart[pl.ds(4 * i, 4)] = sums[i].reshape(4, 16, 128)

    row1 = [
        go(remote(rpart.at[c], rrx.at[n], r1_send.at[n], r1_recv.at[n], (r, c)))
        for n, c in enumerate(peers)
    ]
    for copy in gram2:
        copy.wait_recv()
    for c in range(NCOL):
        for i in range(4):
            out_g[i, pl.ds(8 * c, 8)] = gall[c, :, pl.ds(128 * i, 128)]
    for copy in row1:
        copy.wait_recv()
    total = rpart[k]
    for n in range(len(OFFSETS)):
        total = total + rrx[n]
    rall[k] = total
    row2 = [
        go(remote(rall.at[k], rall.at[k], r2_send.at[n], r2_recv.at[n], (r, c)))
        for n, c in enumerate(peers)
    ]
    for copy in row2:
        copy.wait_recv()
    out_r[...] = rall[...]
    for copy in started:
        copy.wait_send()


def front(cb, tm, cp, rb, tcols, trows):
    any_space = pl.BlockSpec(memory_space=pl.ANY)
    vmem = pl.BlockSpec(memory_space=pltpu.VMEM)
    dma = pltpu.SemaphoreType.DMA
    peers = len(OFFSETS)
    return pl.pallas_call(
        front_kernel,
        out_shape=(
            pltpu.VMEM((NCOL, 16, 128), F32),
            pltpu.VMEM((4, 128, 128), F32),
        ),
        in_specs=[any_space] * 4 + [vmem] * 2,
        out_specs=(vmem, vmem),
        scratch_shapes=[
            pltpu.VMEM((CB, 128, 256), BF16),
            pltpu.VMEM((CB, 64, 256), BF16),
            pltpu.VMEM((4, 128, 128), BF16),
            pltpu.VMEM((HALF, 64, 128), F32),
            pltpu.VMEM((HALF, 64, 128), F32),
            pltpu.VMEM((HALF, 64, 128), F32),
            pltpu.VMEM((3 * SUBS, HC, 64, 128), BF16),
            pltpu.VMEM((3 * SUBS, HC, 32, 128), jnp.int16),
            pltpu.VMEM((3 * SUBS, HC, 64, 128), BF16),
            pltpu.VMEM((3 * SUBS, HC, 32, 128), jnp.int16),
            pltpu.VMEM((CB, 32, 128), jnp.int16),
            pltpu.VMEM((CB, 128, 128), BF16),
            pltpu.VMEM((NCOL, 4, 64, 128), BF16),
            pltpu.VMEM((64, 128, 128), BF16),
            pltpu.VMEM((NCOL, 1, 128), jnp.int32),
            pltpu.SMEM((NCOL, 1, 128), jnp.int32),
            pltpu.VMEM((128, 512), F32),
            pltpu.VMEM((peers, 8, 512), F32),
            pltpu.VMEM((NCOL, 8, 512), F32),
            pltpu.VMEM((NCOL, 16, 128), F32),
            pltpu.VMEM((peers, 16, 128), F32),
            pltpu.VMEM((NCOL, 16, 128), F32),
            dma((2, 8 * SUBS)), dma((3,)),
            dma((4 * SUBS,)), dma((4 * SUBS,)),
        ] + [dma((6 * SUBS,))] * 4 + [dma((8 * SUBS,))] * 2 + [dma((peers,))] * 12,
        compiler_params=pltpu.CompilerParams(
            collective_id=0, has_side_effects=True, vmem_limit_bytes=60 * 1024 * 1024
        ),
    )(cb, tm, cp, rb, tcols, trows)


def back_kernel(rows_s, r_ref, g_ref, rb, cp, nb, nc, cpv, rbv, ncv, proj, sem, out_sem):
    load_cp = pltpu.make_async_copy(cp, cpv, sem.at[0])
    load_cp.start()
    load_rb = pltpu.make_async_copy(rb, rbv, sem.at[1])
    load_rb.start()
    highest = lax.Precision.HIGHEST

    half = 64
    work = []
    for pair in range(2):
        rs = [r_ref[pl.ds(4 * i, 4)].reshape(64, 128) for i in (2 * pair, 2 * pair + 1)]
        curved = []
        for n in range(2):
            middle = lax.dot_general(rs[n], g_ref[2 * pair + n], NN, precision=highest, preferred_element_type=F32)
            curved.append(lax.dot_general(middle, rs[n], NT, precision=highest, preferred_element_type=F32))
        parts = (
            jnp.concatenate(curved, axis=1),
            jnp.concatenate([rs[0][:, :half], rs[1][:, :half]], axis=1),
            jnp.concatenate([rs[0][:, half:], rs[1][:, half:]], axis=1),
        )
        work.append([[part[8 * b:8 * b + 8] for b in range(8)] for part in parts])

    sub = lax.broadcasted_iota(jnp.int32, (8, 128), 0)
    left = lax.broadcasted_iota(jnp.int32, (8, 128), 1) < half
    for step in range(64 // PIVOTS):
        b, o = divmod(PIVOTS * step, 8)
        below = sub >= o + PIVOTS
        for parts in work:
            a = parts[0]
            mult, rows = [], []
            for p in range(PIVOTS):
                k = PIVOTS * step + p
                col = [
                    jnp.take_along_axis(a[n], jnp.where(left, k, half + k), axis=1, mode="promise_in_bounds")
                    for n in range(b, 8)
                ]
                row = [part[b][o + p:o + p + 1] for part in parts]
                for q in range(p):
                    l = mult[q][0][o + p:o + p + 1]
                    col = [cc - mm * l for cc, mm in zip(col, mult[q])]
                    row = [rr - l * uu for rr, uu in zip(row, rows[q])]
                inv = lax.rsqrt(col[0][o + p:o + p + 1])
                mult.append([cc * inv for cc in col])
                rows.append([rr * inv for rr in row])
            for m, part in enumerate(parts):
                for n in range(b, 8):
                    if n == b and o + PIVOTS == 8:
                        continue
                    delta = sum(mult[p][n - b] * rows[p][m] for p in range(PIVOTS))
                    if n == b:
                        delta = jnp.where(below, delta, 0.0)
                    part[n] = part[n] - delta
                if m:
                    done = part[b]
                    for p in range(PIVOTS):
                        done = jnp.where(sub == o + p, rows[p][m], done)
                    part[b] = done

    load_rb.wait()
    for i in range(4):
        lanes = slice(half * (i % 2), half * (i % 2) + half)
        coeff = jnp.concatenate(
            [jnp.concatenate(work[i // 2][m], axis=0)[:, lanes] for m in (1, 2)], axis=1
        )
        hi, lo = split_hi_lo(coeff)
        gram_hi, gram_lo = split_hi_lo(g_ref[i])
        both = lax.dot_general(
            jnp.concatenate([hi, lo], axis=0),
            jnp.concatenate([rbv[i], gram_hi], axis=1),
            NN,
            preferred_element_type=F32,
        )
        both = both[:64] + both[64:]
        nb[i] = both[:, :128]
        hi, lo = split_hi_lo(both[:, 128:] + lax.dot_general(hi, gram_lo, NN, preferred_element_type=F32))
        proj[i] = jnp.concatenate([hi, lo], axis=0)

    load_cp.wait()
    first = lax.broadcasted_iota(jnp.int32, (64, 128), 1) < 64
    outs = [pltpu.make_async_copy(ncv.at[pl.ds(8 * n, 8)], nc.at[pl.ds(8 * n, 8)], out_sem.at[n]) for n in range(8)]
    for n in range(8):
        for t in range(8 * n, 8 * n + 8):
            row = rows_s[t]
            coupling = cpv[t].astype(F32)
            zero = jnp.zeros_like(coupling)
            pair = jnp.concatenate(
                [jnp.where(first, coupling, zero), jnp.where(first, zero, coupling)], axis=0
            ).astype(BF16)
            both = lax.dot_general(proj[jnp.minimum(row, 3)], pair, NN, preferred_element_type=F32)
            live = jnp.where(row < 4, 1.0, 0.0)
            ncv[t] = (both[:64] + both[64:]) * live
        outs[n].start()
    for copy in outs:
        copy.wait()


def back(tile_rows, r_side, gram, rb, cp):
    any_space = pl.BlockSpec(memory_space=pl.ANY)
    vmem = pl.BlockSpec(memory_space=pltpu.VMEM)
    return pl.pallas_call(
        back_kernel,
        out_shape=(
            jax.ShapeDtypeStruct((4, 64, 128), F32),
            jax.ShapeDtypeStruct((64, 64, 128), F32),
        ),
        in_specs=[pl.BlockSpec(memory_space=pltpu.SMEM), vmem, vmem, any_space, any_space],
        out_specs=(vmem, any_space),
        scratch_shapes=[
            pltpu.VMEM((64, 64, 128), BF16),
            pltpu.VMEM((4, 128, 128), BF16),
            pltpu.VMEM((64, 64, 128), F32),
            pltpu.VMEM((4, 128, 128), BF16),
            pltpu.SemaphoreType.DMA((2,)),
            pltpu.SemaphoreType.DMA((8,)),
        ],
        compiler_params=pltpu.CompilerParams(vmem_limit_bytes=60 * 1024 * 1024),
    )(tile_rows, r_side, gram, rb, cp)


def local(row_bases, col_bases, test_matrix, couplings, tile_rows, tile_cols):
    r_side, gram = front(
        col_bases, test_matrix, couplings, row_bases, tile_cols.reshape(1, 64), tile_rows.reshape(1, 64)
    )
    r_side = pltpu.with_memory_space_constraint(r_side, pltpu.VMEM)
    gram = pltpu.with_memory_space_constraint(gram, pltpu.VMEM)
    return back(tile_rows, r_side, gram, row_bases, couplings)


def solution(mesh):
    in_specs = (
        P("rows", None, "cols"),
        P("cols", None, "rows"),
        P("cols", None, "rows"),
        P(("rows", "cols"), None, None),
        P(("rows", "cols")),
        P(("rows", "cols")),
    )
    out_specs = (P("rows", None, "cols"), P(("rows", "cols"), None, None))
    return jax.shard_map(local, mesh=mesh, in_specs=in_specs, out_specs=out_specs, check_vma=False)
```

```python
import functools
import math

import jax
import jax.numpy as jnp
from jax import lax
from jax.experimental import pallas as pl
from jax.experimental.pallas import tpu as pltpu
from jax.sharding import PartitionSpec as P

MESH = pl.DeviceIdType.MESH
F32 = jnp.float32
BF16 = jnp.bfloat16
LEAF = 2048
SCALE = 1.0 / math.sqrt(LEAF)
CB = 48
HALF = 24
CH = 6
SUBS = 2
HC = CH // SUBS
NCOL = 16
STEP = 64
PIVOTS = 8
NT = (((1,), (1,)), ((), ()))
NN = (((1,), (0,)), ((), ()))
OFFSETS = sorted(
    [(dy, dx) for dy in range(4) for dx in range(4) if (dy, dx) != (0, 0)],
    key=lambda o: -min(o[0], 4 - o[0]) - min(o[1], 4 - o[1]),
)


STEPS = 32400.0


def split_hi_lo(value):
    hi = value.astype(BF16)
    return hi, (value - hi.astype(F32)).astype(BF16)


def code(value):
    head = value.astype(BF16)
    base = head.astype(F32)
    rest = (value - base) * pl.reciprocal(jnp.maximum(jnp.abs(base), 1e-30), approx=True)
    steps = jnp.floor(rest * STEPS + 0.5)
    return head, (steps[:32] * 256.0 + steps[32:]).astype(jnp.int32).astype(jnp.int16)


def rest_of(head, word):
    word = word.astype(jnp.int32)
    top = (word + 128) >> 8
    steps = jnp.concatenate([top, word - top * 256], axis=0).astype(F32)
    return jnp.abs(head.astype(F32)) * (steps * (1.0 / STEPS))


def front_kernel(
    cb, tm, cp, rb, tcols, trows, out_r, out_g,
    cbv, tmv, rbv, part, own, prx, zsh, zsw, zrh, zrw, skw, skb, cpl, pairs, idxv, idxs,
    gpart, grx, gall, rpart, rrx, rall,
    ld_sem, misc_sem, pc_send, pc_recv, zs_send, zs_recv, ag_send, ag_recv, fw_send, fw_recv,
    cp_send, cp_recv, ix_send, ix_recv, g1_send, g1_recv, g2_send, g2_recv,
    r1_send, r1_recv, r2_send, r2_recv,
):
    r = lax.axis_index("rows")
    k = lax.axis_index("cols")
    z, h = lax.div(r, 2), lax.rem(r, 2)
    y, x = lax.div(k, 4), lax.rem(k, 4)
    partner = (r + 1 - 2 * h, k)
    along = {q: (lax.rem(z + q, 4) * 2 + h, k) for q in (1, 2, 3)}
    peers = [lax.rem(y + dy, 4) * 4 + lax.rem(x + dx, 4) for dy, dx in OFFSETS]

    def piece(s, q):
        return lax.rem(z + q, 4) * CH + s * HC

    order = [(s, q) for s in range(SUBS) for q in (2, 1, 3, 0)]
    loads = {}
    for n, half in enumerate((1 - h, h)):
        for m, (s, q) in enumerate(order):
            at = pl.ds(half * HALF + piece(s, q), HC)
            a = pltpu.make_async_copy(cb.at[at], cbv.at[at], ld_sem.at[0, 4 * SUBS * n + m])
            b = pltpu.make_async_copy(tm.at[at], tmv.at[at], ld_sem.at[1, 4 * SUBS * n + m])
            a.start()
            b.start()
            loads[n, s, q] = (a, b)
    load_rb = pltpu.make_async_copy(rb, rbv, misc_sem.at[0])
    load_rb.start()
    own_cp = pltpu.make_async_copy(cp.at[pl.ds(4 * k, 4)], cpl.at[k], misc_sem.at[1])
    own_cp.start()

    barrier = pltpu.get_barrier_semaphore()
    for device in [partner, along[1], along[2], along[3]] + [(r, c) for c in peers]:
        pl.semaphore_signal(barrier, inc=1, device_id=device, device_id_type=MESH)

    def sketch(n, s, q, dst):
        for load in loads[n, s, q]:
            load.wait()
        half = (1 - h) if n == 0 else h
        base = half * HALF + piece(s, q)
        for u in range(HC):
            dst[piece(s, q) + u] = (
                lax.dot_general(tmv[base + u], cbv[base + u], NT, preferred_element_type=F32) * SCALE
            )

    def remote(src, dst, send, recv, device):
        return pltpu.make_async_remote_copy(
            src_ref=src, dst_ref=dst, send_sem=send, recv_sem=recv, device_id=device, device_id_type=MESH
        )

    def all_of(ref, sem):
        pltpu.make_async_copy(ref, ref, sem).wait()

    others = pl.ds(0, len(OFFSETS))
    started = []

    def go(copy):
        copy.start()
        started.append(copy)
        return copy

    for s, q in order:
        sketch(0, s, q, part)
    idxv[k] = jnp.concatenate([tcols[...], trows[...]], axis=1)
    load_rb.wait()
    for i in range(4):
        gpart[:, pl.ds(i * 128, 128)] = lax.dot_general(rbv[i], rbv[i], NT, preferred_element_type=F32) * (1.0 / LEAF)
    pl.semaphore_wait(barrier, 4 + len(OFFSETS))
    to_partner = {}
    for m, (s, q) in enumerate(order):
        at = pl.ds(piece(s, q), HC)
        to_partner[s, q] = go(remote(part.at[at], prx.at[at], pc_send.at[m], pc_recv.at[m], partner))
    for n, c in enumerate(peers):
        remote(idxv.at[k], idxv.at[k], ix_send, ix_recv, (r, c)).start()
    for n, c in enumerate(peers):
        remote(gpart.at[pl.ds(8 * c, 8)], grx.at[n], g1_send, g1_recv, (r, c)).start()
    for n, c in enumerate(peers):
        remote(cp.at[pl.ds(4 * c, 4)], cpl.at[k], cp_send, cp_recv, (r, c)).start()

    scatter = {}
    for s, q in order:
        sketch(1, s, q, own)
        to_partner[s, q].wait_recv()
        at = piece(s, q)
        if not q:
            own[pl.ds(at, HC)] = own[pl.ds(at, HC)] + prx[pl.ds(at, HC)]
            continue
        n = 3 * s + q - 1
        for u in range(HC):
            zsh[n, u], zsw[n, u] = code(own[at + u] + prx[at + u])
        scatter[s, q] = (
            go(remote(zsh.at[n], zrh.at[n], zs_send.at[2 * n], zs_recv.at[2 * n], along[q])),
            go(remote(zsw.at[n], zrw.at[n], zs_send.at[2 * n + 1], zs_recv.at[2 * n + 1], along[q])),
        )


    def spread(start, send, recv, n, device):
        heads = skb.at[pl.ds(start, HC), pl.ds(0, 64)]
        words = skw.at[pl.ds(start, HC)]
        return (
            go(remote(heads, heads, send.at[2 * n], recv.at[2 * n], device)),
            go(remote(words, words, send.at[2 * n + 1], recv.at[2 * n + 1], device)),
        )

    def arrived(copies):
        for copy in copies:
            copy.wait_recv()

    def rests(start):
        for u in range(HC):
            skb[start + u, 64:] = rest_of(skb[start + u, :64], skw[start + u]).astype(BF16)

    gather, forwarded = {}, []
    for s in range(SUBS):
        for q in (1, 2, 3):
            arrived(scatter[s, q])
        mine = h * HALF + piece(s, 0)
        for u in range(HC):
            total = own[piece(s, 0) + u]
            for n in range(3 * s, 3 * s + 3):
                head = zrh[n, u]
                total = total + (head.astype(F32) + rest_of(head, zrw[n, u]))
            skb[mine + u, :64], skw[mine + u] = code(total)
        for q in (2, 1, 3):
            gather[s, q] = spread(mine, ag_send, ag_recv, 3 * s + q - 1, along[q])
        forwarded.append((s, 0, spread(mine, fw_send, fw_recv, 4 * s, partner)))
        rests(mine)
    all_of(grx, g1_recv)
    total = gpart[pl.ds(pl.multiple_of(8 * k, 8), 8)]
    for n in range(len(OFFSETS)):
        total = total + grx[n]
    gall[k] = total
    for n, c in enumerate(peers):
        remote(gall.at[k], gall.at[k], g2_send, g2_recv, (r, c)).start()

    for s in range(SUBS):
        for q in (1, 3, 2):
            arrived(gather[s, q])
            start = h * HALF + piece(s, 4 - q)
            forwarded.append((s, 4 - q, spread(start, fw_send, fw_recv, 4 * s + q, partner)))
            rests(start)

    own_cp.wait()
    all_of(idxv.at[others], ix_recv)
    all_of(cpl.at[others], cp_recv)
    to_scalars = pltpu.make_async_copy(idxv, idxs, misc_sem.at[2])
    to_scalars.start()
    first = lax.broadcasted_iota(jnp.int32, (64, 128), 1) < 64

    @pl.loop(0, NCOL)
    def _(c):
        for s in range(4):
            coupling = cpl[c, s].astype(F32)
            zero = jnp.zeros_like(coupling)
            pairs[4 * c + s] = jnp.concatenate(
                [jnp.where(first, coupling, zero), jnp.where(first, zero, coupling)], axis=0
            ).astype(BF16)

    to_scalars.wait()
    for s, q, copies in forwarded:
        arrived(copies)
        rests((1 - h) * HALF + piece(s, q))

    def tiles(n, carry):
        sums = list(carry)
        for m in range(STEP):
            c, s = STEP // 4 * n + m // 4, m % 4
            j = jnp.clip(idxs[c, 0, 4 * k + s] - CB * k, 0, CB - 1)
            row = idxs[c, 0, 64 + 4 * k + s]
            both = lax.dot_general(skb[j], pairs[4 * c + s], NT, preferred_element_type=F32)
            term = both[:64] + both[64:]
            for i in range(4):
                sums[i] = sums[i] + jnp.where(row == i, 1.0, 0.0) * term
        return tuple(sums)

    sums = lax.fori_loop(0, 64 // STEP, tiles, (jnp.zeros((64, 128), F32),) * 4)
    for i in range(4):
        rpart[pl.ds(4 * i, 4)] = sums[i].reshape(4, 16, 128)

    for n, c in enumerate(peers):
        remote(rpart.at[c], rrx.at[n], r1_send, r1_recv, (r, c)).start()
    all_of(gall.at[others], g2_recv)
    for c in range(NCOL):
        for i in range(4):
            out_g[i, pl.ds(8 * c, 8)] = gall[c, :, pl.ds(128 * i, 128)]
    for copy in started:
        copy.wait_send()
    all_of(idxv.at[others], ix_send)
    all_of(cpl.at[others], cp_send)
    all_of(grx, g1_send)
    all_of(gall.at[others], g2_send)
    all_of(rrx, r1_recv)
    total = rpart[k]
    for n in range(len(OFFSETS)):
        total = total + rrx[n]
    rall[k] = total
    for n, c in enumerate(peers):
        remote(rall.at[k], rall.at[k], r2_send, r2_recv, (r, c)).start()
    all_of(rrx, r1_send)
    all_of(rall.at[others], r2_recv)
    out_r[...] = rall[...]
    all_of(rall.at[others], r2_send)


def front(cb, tm, cp, rb, tcols, trows):
    any_space = pl.BlockSpec(memory_space=pl.ANY)
    vmem = pl.BlockSpec(memory_space=pltpu.VMEM)
    dma = pltpu.SemaphoreType.DMA
    peers = len(OFFSETS)
    return pl.pallas_call(
        front_kernel,
        out_shape=(
            pltpu.VMEM((NCOL, 16, 128), F32),
            pltpu.VMEM((4, 128, 128), F32),
        ),
        in_specs=[any_space] * 4 + [vmem] * 2,
        out_specs=(vmem, vmem),
        scratch_shapes=[
            pltpu.VMEM((CB, 128, 256), BF16),
            pltpu.VMEM((CB, 64, 256), BF16),
            pltpu.VMEM((4, 128, 128), BF16),
            pltpu.VMEM((HALF, 64, 128), F32),
            pltpu.VMEM((HALF, 64, 128), F32),
            pltpu.VMEM((HALF, 64, 128), F32),
            pltpu.VMEM((3 * SUBS, HC, 64, 128), BF16),
            pltpu.VMEM((3 * SUBS, HC, 32, 128), jnp.int16),
            pltpu.VMEM((3 * SUBS, HC, 64, 128), BF16),
            pltpu.VMEM((3 * SUBS, HC, 32, 128), jnp.int16),
            pltpu.VMEM((CB, 32, 128), jnp.int16),
            pltpu.VMEM((CB, 128, 128), BF16),
            pltpu.VMEM((NCOL, 4, 64, 128), BF16),
            pltpu.VMEM((64, 128, 128), BF16),
            pltpu.VMEM((NCOL, 1, 128), jnp.int32),
            pltpu.SMEM((NCOL, 1, 128), jnp.int32),
            pltpu.VMEM((128, 512), F32),
            pltpu.VMEM((peers, 8, 512), F32),
            pltpu.VMEM((NCOL, 8, 512), F32),
            pltpu.VMEM((NCOL, 16, 128), F32),
            pltpu.VMEM((peers, 16, 128), F32),
            pltpu.VMEM((NCOL, 16, 128), F32),
            dma((2, 8 * SUBS)), dma((3,)),
            dma((4 * SUBS,)), dma((4 * SUBS,)),
        ] + [dma((6 * SUBS,))] * 4 + [dma((8 * SUBS,))] * 2 + [dma] * 12,
        compiler_params=pltpu.CompilerParams(
            collective_id=0, has_side_effects=True, vmem_limit_bytes=60 * 1024 * 1024
        ),
    )(cb, tm, cp, rb, tcols, trows)


def back_kernel(rows_s, r_ref, g_ref, rb, cp, nb, nc, cpv, rbv, ncv, proj, sem, out_sem):
    load_cp = pltpu.make_async_copy(cp, cpv, sem.at[0])
    load_cp.start()
    load_rb = pltpu.make_async_copy(rb, rbv, sem.at[1])
    load_rb.start()
    highest = lax.Precision.HIGHEST

    half = 64
    work = []
    for pair in range(2):
        rs = [r_ref[pl.ds(4 * i, 4)].reshape(64, 128) for i in (2 * pair, 2 * pair + 1)]
        curved = []
        for n in range(2):
            middle = lax.dot_general(rs[n], g_ref[2 * pair + n], NN, precision=highest, preferred_element_type=F32)
            curved.append(lax.dot_general(middle, rs[n], NT, precision=highest, preferred_element_type=F32))
        parts = (
            jnp.concatenate(curved, axis=1),
            jnp.concatenate([rs[0][:, :half], rs[1][:, :half]], axis=1),
            jnp.concatenate([rs[0][:, half:], rs[1][:, half:]], axis=1),
        )
        work.append([[part[8 * b:8 * b + 8] for b in range(8)] for part in parts])

    sub = lax.broadcasted_iota(jnp.int32, (8, 128), 0)
    left = lax.broadcasted_iota(jnp.int32, (8, 128), 1) < half
    for step in range(64 // PIVOTS):
        b, o = divmod(PIVOTS * step, 8)
        below = sub >= o + PIVOTS
        for parts in work:
            a = parts[0]
            mult, rows = [], []
            for p in range(PIVOTS):
                k = PIVOTS * step + p
                col = [
                    jnp.take_along_axis(a[n], jnp.where(left, k, half + k), axis=1, mode="promise_in_bounds")
                    for n in range(b, 8)
                ]
                row = [part[b][o + p:o + p + 1] for part in parts]
                for q in range(p):
                    l = mult[q][0][o + p:o + p + 1]
                    col = [cc - mm * l for cc, mm in zip(col, mult[q])]
                    row = [rr - l * uu for rr, uu in zip(row, rows[q])]
                inv = lax.rsqrt(col[0][o + p:o + p + 1])
                mult.append([cc * inv for cc in col])
                rows.append([rr * inv for rr in row])
            for m, part in enumerate(parts):
                for n in range(b, 8):
                    if n == b and o + PIVOTS == 8:
                        continue
                    delta = sum(mult[p][n - b] * rows[p][m] for p in range(PIVOTS))
                    if n == b:
                        delta = jnp.where(below, delta, 0.0)
                    part[n] = part[n] - delta
                if m:
                    done = part[b]
                    for p in range(PIVOTS):
                        done = jnp.where(sub == o + p, rows[p][m], done)
                    part[b] = done

    load_rb.wait()
    for i in range(4):
        lanes = slice(half * (i % 2), half * (i % 2) + half)
        coeff = jnp.concatenate(
            [jnp.concatenate(work[i // 2][m], axis=0)[:, lanes] for m in (1, 2)], axis=1
        )
        hi, lo = split_hi_lo(coeff)
        gram_hi, gram_lo = split_hi_lo(g_ref[i])
        both = lax.dot_general(
            jnp.concatenate([hi, lo], axis=0),
            jnp.concatenate([rbv[i], gram_hi], axis=1),
            NN,
            preferred_element_type=F32,
        )
        both = both[:64] + both[64:]
        nb[i] = both[:, :128]
        hi, lo = split_hi_lo(both[:, 128:] + lax.dot_general(hi, gram_lo, NN, preferred_element_type=F32))
        proj[i] = jnp.concatenate([hi, lo], axis=0)

    load_cp.wait()
    first = lax.broadcasted_iota(jnp.int32, (64, 128), 1) < 64
    outs = [pltpu.make_async_copy(ncv.at[pl.ds(8 * n, 8)], nc.at[pl.ds(8 * n, 8)], out_sem.at[n]) for n in range(8)]
    for n in range(8):
        for t in range(8 * n, 8 * n + 8):
            row = rows_s[t]
            coupling = cpv[t].astype(F32)
            zero = jnp.zeros_like(coupling)
            pair = jnp.concatenate(
                [jnp.where(first, coupling, zero), jnp.where(first, zero, coupling)], axis=0
            ).astype(BF16)
            both = lax.dot_general(proj[jnp.minimum(row, 3)], pair, NN, preferred_element_type=F32)
            live = jnp.where(row < 4, 1.0, 0.0)
            ncv[t] = (both[:64] + both[64:]) * live
        outs[n].start()
    for copy in outs:
        copy.wait()


def back(tile_rows, r_side, gram, rb, cp):
    any_space = pl.BlockSpec(memory_space=pl.ANY)
    vmem = pl.BlockSpec(memory_space=pltpu.VMEM)
    return pl.pallas_call(
        back_kernel,
        out_shape=(
            jax.ShapeDtypeStruct((4, 64, 128), F32),
            jax.ShapeDtypeStruct((64, 64, 128), F32),
        ),
        in_specs=[pl.BlockSpec(memory_space=pltpu.SMEM), vmem, vmem, any_space, any_space],
        out_specs=(vmem, any_space),
        scratch_shapes=[
            pltpu.VMEM((64, 64, 128), BF16),
            pltpu.VMEM((4, 128, 128), BF16),
            pltpu.VMEM((64, 64, 128), F32),
            pltpu.VMEM((4, 128, 128), BF16),
            pltpu.SemaphoreType.DMA((2,)),
            pltpu.SemaphoreType.DMA((8,)),
        ],
        compiler_params=pltpu.CompilerParams(vmem_limit_bytes=60 * 1024 * 1024),
    )(tile_rows, r_side, gram, rb, cp)


def local(row_bases, col_bases, test_matrix, couplings, tile_rows, tile_cols):
    r_side, gram = front(
        col_bases, test_matrix, couplings, row_bases, tile_cols.reshape(1, 64), tile_rows.reshape(1, 64)
    )
    r_side = pltpu.with_memory_space_constraint(r_side, pltpu.VMEM)
    gram = pltpu.with_memory_space_constraint(gram, pltpu.VMEM)
    return back(tile_rows, r_side, gram, row_bases, couplings)


def solution(mesh):
    in_specs = (
        P("rows", None, "cols"),
        P("cols", None, "rows"),
        P("cols", None, "rows"),
        P(("rows", "cols"), None, None),
        P(("rows", "cols")),
        P(("rows", "cols")),
    )
    out_specs = (P("rows", None, "cols"), P(("rows", "cols"), None, None))
    return jax.shard_map(local, mesh=mesh, in_specs=in_specs, out_specs=out_specs, check_vma=False)
```

```python
import functools
import math

import jax
import jax.numpy as jnp
from jax import lax
from jax.experimental import pallas as pl
from jax.experimental.pallas import tpu as pltpu
from jax.sharding import PartitionSpec as P

MESH = pl.DeviceIdType.MESH
F32 = jnp.float32
BF16 = jnp.bfloat16
LEAF = 2048
SCALE = 1.0 / math.sqrt(LEAF)
CB = 48
HALF = 24
CH = 6
SUBS = 2
HC = CH // SUBS
NCOL = 16
STEP = 64
PIVOTS = 8
NT = (((1,), (1,)), ((), ()))
NN = (((1,), (0,)), ((), ()))
OFFSETS = sorted(
    [(dy, dx) for dy in range(4) for dx in range(4) if (dy, dx) != (0, 0)],
    key=lambda o: -min(o[0], 4 - o[0]) - min(o[1], 4 - o[1]),
)


STEPS = 32400.0


def split_hi_lo(value):
    hi = value.astype(BF16)
    return hi, (value - hi.astype(F32)).astype(BF16)


def code(value):
    head = value.astype(BF16)
    base = head.astype(F32)
    rest = (value - base) * pl.reciprocal(jnp.maximum(jnp.abs(base), 1e-30), approx=True)
    steps = jnp.floor(rest * STEPS + 0.5)
    return head, (steps[:32] * 256.0 + steps[32:]).astype(jnp.int32).astype(jnp.int16)


def rest_of(head, word):
    word = word.astype(jnp.int32)
    top = (word + 128) >> 8
    steps = jnp.concatenate([top, word - top * 256], axis=0).astype(F32)
    return jnp.abs(head.astype(F32)) * (steps * (1.0 / STEPS))


def front_kernel(
    cb, tm, cp, rb, tcols, trows, out_r, out_g,
    cbv, tmv, rbv, part, own, prx, zsh, zsw, zrh, zrw, skw, skb, cpl, pairs, idxv, idxs,
    gpart, grx, gall, rpart, rrx, rall,
    ld_sem, misc_sem, pc_send, pc_recv, zs_send, zs_recv, ag_send, ag_recv, fw_send, fw_recv,
    cp_send, cp_recv, ix_send, ix_recv, g1_send, g1_recv, g2_send, g2_recv,
    r1_send, r1_recv, r2_send, r2_recv,
):
    r = lax.axis_index("rows")
    k = lax.axis_index("cols")
    z, h = lax.div(r, 2), lax.rem(r, 2)
    y, x = lax.div(k, 4), lax.rem(k, 4)
    partner = (r + 1 - 2 * h, k)
    along = {q: (lax.rem(z + q, 4) * 2 + h, k) for q in (1, 2, 3)}
    peers = [lax.rem(y + dy, 4) * 4 + lax.rem(x + dx, 4) for dy, dx in OFFSETS]

    def piece(s, q):
        return lax.rem(z + q, 4) * CH + s * HC

    order = [(s, q) for s in range(SUBS) for q in (2, 1, 3, 0)]
    loads = {}
    for n, half in enumerate((1 - h, h)):
        for m, q in enumerate((2, 1, 3, 0)):
            at = pl.ds(half * HALF + piece(0, q), CH)
            a = pltpu.make_async_copy(cb.at[at], cbv.at[at], ld_sem.at[0, 4 * n + m])
            b = pltpu.make_async_copy(tm.at[at], tmv.at[at], ld_sem.at[1, 4 * n + m])
            a.start()
            b.start()
            loads[n, q] = (a, b)
    load_rb = pltpu.make_async_copy(rb, rbv, misc_sem.at[0])
    load_rb.start()
    own_cp = pltpu.make_async_copy(cp.at[pl.ds(4 * k, 4)], cpl.at[k], misc_sem.at[1])
    own_cp.start()

    barrier = pltpu.get_barrier_semaphore()
    for device in [partner, along[1], along[2], along[3]] + [(r, c) for c in peers]:
        pl.semaphore_signal(barrier, inc=1, device_id=device, device_id_type=MESH)

    def sketch(n, s, q, dst):
        for load in loads[n, q] if s == 0 else ():
            load.wait()
        half = (1 - h) if n == 0 else h
        base = half * HALF + piece(s, q)
        for u in range(HC):
            dst[piece(s, q) + u] = (
                lax.dot_general(tmv[base + u], cbv[base + u], NT, preferred_element_type=F32) * SCALE
            )

    def remote(src, dst, send, recv, device):
        return pltpu.make_async_remote_copy(
            src_ref=src, dst_ref=dst, send_sem=send, recv_sem=recv, device_id=device, device_id_type=MESH
        )

    def all_of(ref, sem):
        pltpu.make_async_copy(ref, ref, sem).wait()

    others = pl.ds(0, len(OFFSETS))
    started = []

    def go(copy):
        copy.start()
        started.append(copy)
        return copy

    for s, q in order:
        sketch(0, s, q, part)
    idxv[k] = jnp.concatenate([tcols[...], trows[...]], axis=1)
    load_rb.wait()
    for i in range(4):
        gpart[:, pl.ds(i * 128, 128)] = lax.dot_general(rbv[i], rbv[i], NT, preferred_element_type=F32) * (1.0 / LEAF)
    pl.semaphore_wait(barrier, 4 + len(OFFSETS))
    to_partner = {}
    for m, (s, q) in enumerate(order):
        at = pl.ds(piece(s, q), HC)
        to_partner[s, q] = go(remote(part.at[at], prx.at[at], pc_send.at[m], pc_recv.at[m], partner))
    for n, c in enumerate(peers):
        remote(idxv.at[k], idxv.at[k], ix_send, ix_recv, (r, c)).start()
    for n, c in enumerate(peers):
        remote(gpart.at[pl.ds(8 * c, 8)], grx.at[n], g1_send, g1_recv, (r, c)).start()
    for n, c in enumerate(peers):
        remote(cp.at[pl.ds(4 * c, 4)], cpl.at[k], cp_send, cp_recv, (r, c)).start()

    for s, q in order:
        sketch(1, s, q, own)
        to_partner[s, q].wait_recv()
        at = piece(s, q)
        if not q:
            own[pl.ds(at, HC)] = own[pl.ds(at, HC)] + prx[pl.ds(at, HC)]
            continue
        n = 3 * s + q - 1
        for u in range(HC):
            zsh[n, u], zsw[n, u] = code(own[at + u] + prx[at + u])
        go(remote(zsh.at[n], zrh.at[n], zs_send.at[2 * n], zs_recv.at[2 * s], along[q]))
        go(remote(zsw.at[n], zrw.at[n], zs_send.at[2 * n + 1], zs_recv.at[2 * s + 1], along[q]))


    def spread(start, send, recv, n, m, device):
        heads = skb.at[pl.ds(start, HC), pl.ds(0, 64)]
        words = skw.at[pl.ds(start, HC)]
        return (
            go(remote(heads, heads, send.at[2 * n], recv.at[2 * m], device)),
            go(remote(words, words, send.at[2 * n + 1], recv.at[2 * m + 1], device)),
        )

    def arrived(copies):
        for copy in copies:
            copy.wait_recv()

    def rests(start):
        for u in range(HC):
            skb[start + u, 64:] = rest_of(skb[start + u, :64], skw[start + u]).astype(BF16)

    gather = {}
    for s in range(SUBS):
        all_of(zrh.at[pl.ds(3 * s, 3)], zs_recv.at[2 * s])
        all_of(zrw.at[pl.ds(3 * s, 3)], zs_recv.at[2 * s + 1])
        mine = h * HALF + piece(s, 0)
        for u in range(HC):
            total = own[piece(s, 0) + u]
            for n in range(3 * s, 3 * s + 3):
                head = zrh[n, u]
                total = total + (head.astype(F32) + rest_of(head, zrw[n, u]))
            skb[mine + u, :64], skw[mine + u] = code(total)
        for q in (2, 1, 3):
            gather[s, q] = spread(mine, ag_send, ag_recv, 3 * s + q - 1, 3 * s + q - 1, along[q])
        spread(mine, fw_send, fw_recv, 4 * s, 0, partner)
        rests(mine)
    all_of(grx, g1_recv)
    total = gpart[pl.ds(pl.multiple_of(8 * k, 8), 8)]
    for n in range(len(OFFSETS)):
        total = total + grx[n]
    gall[k] = total
    for n, c in enumerate(peers):
        remote(gall.at[k], gall.at[k], g2_send, g2_recv, (r, c)).start()

    for s in range(SUBS):
        for q in (1, 3, 2):
            arrived(gather[s, q])
            start = h * HALF + piece(s, 4 - q)
            spread(start, fw_send, fw_recv, 4 * s + q, 0, partner)
            rests(start)

    own_cp.wait()
    all_of(idxv.at[others], ix_recv)
    all_of(cpl.at[others], cp_recv)
    to_scalars = pltpu.make_async_copy(idxv, idxs, misc_sem.at[2])
    to_scalars.start()
    first = lax.broadcasted_iota(jnp.int32, (64, 128), 1) < 64

    @pl.loop(0, NCOL)
    def _(c):
        for s in range(4):
            coupling = cpl[c, s].astype(F32)
            zero = jnp.zeros_like(coupling)
            pairs[4 * c + s] = jnp.concatenate(
                [jnp.where(first, coupling, zero), jnp.where(first, zero, coupling)], axis=0
            ).astype(BF16)

    to_scalars.wait()
    all_of(skb.at[pl.ds(0, HALF), pl.ds(0, 64)], fw_recv.at[0])
    all_of(skw.at[pl.ds(0, HALF)], fw_recv.at[1])
    for s, q in order:
        rests((1 - h) * HALF + piece(s, q))

    def tiles(n, carry):
        sums = list(carry)
        for m in range(STEP):
            c, s = STEP // 4 * n + m // 4, m % 4
            j = jnp.clip(idxs[c, 0, 4 * k + s] - CB * k, 0, CB - 1)
            row = idxs[c, 0, 64 + 4 * k + s]
            both = lax.dot_general(skb[j], pairs[4 * c + s], NT, preferred_element_type=F32)
            term = both[:64] + both[64:]
            for i in range(4):
                sums[i] = sums[i] + jnp.where(row == i, 1.0, 0.0) * term
        return tuple(sums)

    sums = lax.fori_loop(0, 64 // STEP, tiles, (jnp.zeros((64, 128), F32),) * 4)
    for i in range(4):
        rpart[pl.ds(4 * i, 4)] = sums[i].reshape(4, 16, 128)

    for n, c in enumerate(peers):
        remote(rpart.at[c], rrx.at[n], r1_send, r1_recv, (r, c)).start()
    all_of(gall.at[others], g2_recv)
    for c in range(NCOL):
        for i in range(4):
            out_g[i, pl.ds(8 * c, 8)] = gall[c, :, pl.ds(128 * i, 128)]
    for copy in started:
        copy.wait_send()
    all_of(idxv.at[others], ix_send)
    all_of(cpl.at[others], cp_send)
    all_of(grx, g1_send)
    all_of(gall.at[others], g2_send)
    all_of(rrx, r1_recv)
    total = rpart[k]
    for n in range(len(OFFSETS)):
        total = total + rrx[n]
    rall[k] = total
    for n, c in enumerate(peers):
        remote(rall.at[k], rall.at[k], r2_send, r2_recv, (r, c)).start()
    all_of(rrx, r1_send)
    all_of(rall.at[others], r2_recv)
    out_r[...] = rall[...]
    all_of(rall.at[others], r2_send)


def front(cb, tm, cp, rb, tcols, trows):
    any_space = pl.BlockSpec(memory_space=pl.ANY)
    vmem = pl.BlockSpec(memory_space=pltpu.VMEM)
    dma = pltpu.SemaphoreType.DMA
    peers = len(OFFSETS)
    return pl.pallas_call(
        front_kernel,
        out_shape=(
            pltpu.VMEM((NCOL, 16, 128), F32),
            pltpu.VMEM((4, 128, 128), F32),
        ),
        in_specs=[any_space] * 4 + [vmem] * 2,
        out_specs=(vmem, vmem),
        scratch_shapes=[
            pltpu.VMEM((CB, 128, 256), BF16),
            pltpu.VMEM((CB, 64, 256), BF16),
            pltpu.VMEM((4, 128, 128), BF16),
            pltpu.VMEM((HALF, 64, 128), F32),
            pltpu.VMEM((HALF, 64, 128), F32),
            pltpu.VMEM((HALF, 64, 128), F32),
            pltpu.VMEM((3 * SUBS, HC, 64, 128), BF16),
            pltpu.VMEM((3 * SUBS, HC, 32, 128), jnp.int16),
            pltpu.VMEM((3 * SUBS, HC, 64, 128), BF16),
            pltpu.VMEM((3 * SUBS, HC, 32, 128), jnp.int16),
            pltpu.VMEM((CB, 32, 128), jnp.int16),
            pltpu.VMEM((CB, 128, 128), BF16),
            pltpu.VMEM((NCOL, 4, 64, 128), BF16),
            pltpu.VMEM((64, 128, 128), BF16),
            pltpu.VMEM((NCOL, 1, 128), jnp.int32),
            pltpu.SMEM((NCOL, 1, 128), jnp.int32),
            pltpu.VMEM((128, 512), F32),
            pltpu.VMEM((peers, 8, 512), F32),
            pltpu.VMEM((NCOL, 8, 512), F32),
            pltpu.VMEM((NCOL, 16, 128), F32),
            pltpu.VMEM((peers, 16, 128), F32),
            pltpu.VMEM((NCOL, 16, 128), F32),
            dma((2, 8)), dma((3,)),
            dma((4 * SUBS,)), dma((4 * SUBS,)),
        ] + [dma((6 * SUBS,))] * 4 + [dma((8 * SUBS,))] * 2 + [dma] * 12,
        compiler_params=pltpu.CompilerParams(
            collective_id=0, has_side_effects=True, vmem_limit_bytes=60 * 1024 * 1024
        ),
    )(cb, tm, cp, rb, tcols, trows)


def back_kernel(rows_s, r_ref, g_ref, rb, cp, nb, nc, cpv, rbv, ncv, proj, sem, out_sem):
    load_cp = pltpu.make_async_copy(cp, cpv, sem.at[0])
    load_cp.start()
    load_rb = pltpu.make_async_copy(rb, rbv, sem.at[1])
    load_rb.start()
    highest = lax.Precision.HIGHEST

    half = 64
    work = []
    for pair in range(2):
        rs = [r_ref[pl.ds(4 * i, 4)].reshape(64, 128) for i in (2 * pair, 2 * pair + 1)]
        curved = []
        for n in range(2):
            middle = lax.dot_general(rs[n], g_ref[2 * pair + n], NN, precision=highest, preferred_element_type=F32)
            curved.append(lax.dot_general(middle, rs[n], NT, precision=highest, preferred_element_type=F32))
        parts = (
            jnp.concatenate(curved, axis=1),
            jnp.concatenate([rs[0][:, :half], rs[1][:, :half]], axis=1),
            jnp.concatenate([rs[0][:, half:], rs[1][:, half:]], axis=1),
        )
        work.append([[part[8 * b:8 * b + 8] for b in range(8)] for part in parts])

    sub = lax.broadcasted_iota(jnp.int32, (8, 128), 0)
    left = lax.broadcasted_iota(jnp.int32, (8, 128), 1) < half
    for step in range(64 // PIVOTS):
        b, o = divmod(PIVOTS * step, 8)
        below = sub >= o + PIVOTS
        for parts in work:
            a = parts[0]
            mult, rows = [], []
            for p in range(PIVOTS):
                k = PIVOTS * step + p
                col = [
                    jnp.take_along_axis(a[n], jnp.where(left, k, half + k), axis=1, mode="promise_in_bounds")
                    for n in range(b, 8)
                ]
                row = [part[b][o + p:o + p + 1] for part in parts]
                for q in range(p):
                    l = mult[q][0][o + p:o + p + 1]
                    col = [cc - mm * l for cc, mm in zip(col, mult[q])]
                    row = [rr - l * uu for rr, uu in zip(row, rows[q])]
                inv = lax.rsqrt(col[0][o + p:o + p + 1])
                mult.append([cc * inv for cc in col])
                rows.append([rr * inv for rr in row])
            for m, part in enumerate(parts):
                for n in range(b, 8):
                    if n == b and o + PIVOTS == 8:
                        continue
                    delta = sum(mult[p][n - b] * rows[p][m] for p in range(PIVOTS))
                    if n == b:
                        delta = jnp.where(below, delta, 0.0)
                    part[n] = part[n] - delta
                if m:
                    done = part[b]
                    for p in range(PIVOTS):
                        done = jnp.where(sub == o + p, rows[p][m], done)
                    part[b] = done

    load_rb.wait()
    for i in range(4):
        lanes = slice(half * (i % 2), half * (i % 2) + half)
        coeff = jnp.concatenate(
            [jnp.concatenate(work[i // 2][m], axis=0)[:, lanes] for m in (1, 2)], axis=1
        )
        hi, lo = split_hi_lo(coeff)
        gram_hi, gram_lo = split_hi_lo(g_ref[i])
        both = lax.dot_general(
            jnp.concatenate([hi, lo], axis=0),
            jnp.concatenate([rbv[i], gram_hi], axis=1),
            NN,
            preferred_element_type=F32,
        )
        both = both[:64] + both[64:]
        nb[i] = both[:, :128]
        hi, lo = split_hi_lo(both[:, 128:] + lax.dot_general(hi, gram_lo, NN, preferred_element_type=F32))
        proj[i] = jnp.concatenate([hi, lo], axis=0)

    load_cp.wait()
    first = lax.broadcasted_iota(jnp.int32, (64, 128), 1) < 64
    outs = [pltpu.make_async_copy(ncv.at[pl.ds(8 * n, 8)], nc.at[pl.ds(8 * n, 8)], out_sem.at[n]) for n in range(8)]
    for n in range(8):
        for t in range(8 * n, 8 * n + 8):
            row = rows_s[t]
            coupling = cpv[t].astype(F32)
            zero = jnp.zeros_like(coupling)
            pair = jnp.concatenate(
                [jnp.where(first, coupling, zero), jnp.where(first, zero, coupling)], axis=0
            ).astype(BF16)
            both = lax.dot_general(proj[jnp.minimum(row, 3)], pair, NN, preferred_element_type=F32)
            live = jnp.where(row < 4, 1.0, 0.0)
            ncv[t] = (both[:64] + both[64:]) * live
        outs[n].start()
    for copy in outs:
        copy.wait()


def back(tile_rows, r_side, gram, rb, cp):
    any_space = pl.BlockSpec(memory_space=pl.ANY)
    vmem = pl.BlockSpec(memory_space=pltpu.VMEM)
    return pl.pallas_call(
        back_kernel,
        out_shape=(
            jax.ShapeDtypeStruct((4, 64, 128), F32),
            jax.ShapeDtypeStruct((64, 64, 128), F32),
        ),
        in_specs=[pl.BlockSpec(memory_space=pltpu.SMEM), vmem, vmem, any_space, any_space],
        out_specs=(vmem, any_space),
        scratch_shapes=[
            pltpu.VMEM((64, 64, 128), BF16),
            pltpu.VMEM((4, 128, 128), BF16),
            pltpu.VMEM((64, 64, 128), F32),
            pltpu.VMEM((4, 128, 128), BF16),
            pltpu.SemaphoreType.DMA((2,)),
            pltpu.SemaphoreType.DMA((8,)),
        ],
        compiler_params=pltpu.CompilerParams(vmem_limit_bytes=60 * 1024 * 1024),
    )(tile_rows, r_side, gram, rb, cp)


def local(row_bases, col_bases, test_matrix, couplings, tile_rows, tile_cols):
    r_side, gram = front(
        col_bases, test_matrix, couplings, row_bases, tile_cols.reshape(1, 64), tile_rows.reshape(1, 64)
    )
    r_side = pltpu.with_memory_space_constraint(r_side, pltpu.VMEM)
    gram = pltpu.with_memory_space_constraint(gram, pltpu.VMEM)
    return back(tile_rows, r_side, gram, row_bases, couplings)


def solution(mesh):
    in_specs = (
        P("rows", None, "cols"),
        P("cols", None, "rows"),
        P("cols", None, "rows"),
        P(("rows", "cols"), None, None),
        P(("rows", "cols")),
        P(("rows", "cols")),
    )
    out_specs = (P("rows", None, "cols"), P(("rows", "cols"), None, None))
    return jax.shard_map(local, mesh=mesh, in_specs=in_specs, out_specs=out_specs, check_vma=False)
```
